32 devices in a mesh: chan: 4 (over z), sec: 8 (over y, x, core).
Axes of the slice: x: 2, y: 2, z: 4, core: 2. Of those that a mesh axis runs over, the one named last changes fastest.
Arguments:
- psi: bfloat16 [192, 4, 256, 256], P('sec'), may hold values from -6 to 6
- mpo: float32 [4, 4, 4], P('chan'), may hold values from -1.5 to 1.5
- left_env: bfloat16 [4, 64, 256, 256], P('chan', 'sec'), may hold values from -0.375 to 0.375
- right_env: bfloat16 [4, 192, 256, 256], P('chan', 'sec'), may hold values from -0.375 to 0.375
- left_dims: int32 [64], P('sec'), may hold values from 128 to 256, as said below
- right_dims: int32 [192], P('sec'), may hold values from 128 to 256, as said below
- dest_owner: int32 [192, 1], P('sec'), may hold values from 0 to 7, as said below
- left_slot: int32 [192], P('sec'), may hold values from 0 to 7
Outputs:
- h_psi: bfloat16 [192, 4, 256, 256], P('sec', None, 'chan')
The draws below stay inside these ranges and needn't reach their ends.
Inputs may be any that keep to these rules, and one draw needn't show every extreme that they name: `dest_owner`: each device's 24 blocks name one owner at most 3 times; in every draw some owner is named exactly 3 times by the blocks of every device. `left_dims`: multiples of 128; both bounds are reached. `right_dims`: multiples of 128; both bounds are reached.
All inputs are finite; a program needn't handle non-finite values.
Results may differ from the reference program's by a relative error of at most 0.014.
Values may be sent and summed in bfloat16 or wider, within the bound.
No kernel may reach another device: no remote copies, remote signals or barrier semaphores. Data moves between devices by JAX's collectives and lax.ppermute only.
A program may use at most 192 MiB of HBM per device.

```python
import jax
import jax.numpy as jnp
from jax import lax

UNIT = 128
B = 256
P_SIZE = 4
BLK_DEV = 24
LSEC_DEV = 8
CAP = 3
NB = 192
LSECT = 64
W = 4
N_CHAN = 4


def draw_widths(key, count):
    units = jax.random.randint(key, (count,), 1, B // UNIT + 1)
    widths = (UNIT * units).astype(jnp.int32)
    return widths.at[0].set(B).at[1].set(UNIT)


def draw_left_dims(key, part):
    return draw_widths(jax.random.fold_in(key, 101), LSECT)


def draw_right_dims(key, part):
    return draw_widths(jax.random.fold_in(key, 202), NB)


def draw_dest_owner(key, part):
    owners = NB // BLK_DEV
    busiest = jax.random.randint(jax.random.fold_in(key, 7), (), 0, owners)
    labels = jnp.repeat(jnp.arange(owners, dtype=jnp.int32), CAP)

    def draw_row(number):
        row_key = jax.random.fold_in(jax.random.fold_in(key, 303), number)
        ranks = jax.random.permutation(row_key, owners * CAP).astype(jnp.int32)
        scores = ranks + jnp.where(labels == busiest, owners * CAP, 0).astype(jnp.int32)
        picked = jnp.argsort(-scores, stable=True)[:BLK_DEV]
        chosen = labels[picked]
        return jax.random.permutation(jax.random.fold_in(row_key, 3), chosen)
    table = jax.vmap(draw_row)(jnp.arange(owners, dtype=jnp.int32))
    return table.reshape(NB, 1).astype(jnp.int32)


def plant(values, own_key, least, largest):
    longest = values.shape.index(max(values.shape))
    spots = []
    for shift in (0, 1):
        where = [jax.random.randint(jax.random.fold_in(own_key, axis), (), 0, length) for axis, length in enumerate(values.shape)]
        where[longest] = (where[longest] + shift) % values.shape[longest]
        spots.append(tuple(where))
    return values.at[spots[0]].set(least).at[spots[1]].set(largest)


def block_levels(stream_key, extent, split, smallest, high):
    loudness, own = 1.0, jax.random.fold_in(stream_key, 6)
    for axis_at, blocks in split:
        steps = jnp.exp(jax.random.uniform(jax.random.fold_in(own, axis_at), (blocks,), jnp.float32, smallest / len(split), high / len(split)))
        loudness = loudness * jnp.repeat(steps, extent[axis_at] // blocks).reshape([-1 if axis == axis_at else 1 for axis in range(len(extent))])
    return loudness


def gaussian(own_key, shape, width, reach, cuts=(), kind=jnp.bfloat16):
    entries = jax.random.normal(own_key, shape, jnp.float32) * width
    if len(cuts) > 0:
        entries = block_levels(own_key, shape, cuts, -0.22, 0.18) * entries
    return jnp.clip(entries, min=-reach, max=reach).astype(kind)


def setup_inputs(seed: int = 0) -> dict:
    key_of = jax.random.split(jax.random.key(seed), 9)
    return {
        "psi": gaussian(key_of[0], (NB, P_SIZE, B, B), 1.0, 6.0, ((0, 8),)),
        "mpo": gaussian(key_of[1], (W, P_SIZE, P_SIZE), (P_SIZE * W) ** -0.5, 1.5, ((0, 4),), jnp.float32),
        "left_env": gaussian(key_of[2], (W, LSECT, B, B), B ** -0.5, 0.375, ((0, 4), (1, 8))),
        "right_env": gaussian(key_of[3], (W, NB, B, B), B ** -0.5, 0.375, ((0, 4), (1, 8))),
        "left_dims": draw_left_dims(jax.random.fold_in(key_of[8], 71), 0),
        "right_dims": draw_right_dims(jax.random.fold_in(key_of[8], 71), 0),
        "dest_owner": draw_dest_owner(jax.random.fold_in(key_of[8], 71), 0),
        "left_slot": plant(jax.random.randint(key_of[7], (NB,), 0, LSEC_DEV), jax.random.fold_in(key_of[7], 1), 0, LSEC_DEV - 1).astype(jnp.int32),
    }


def reference(psi, mpo, left_env, right_env, left_dims, right_dims, dest_owner, left_slot):
    places = jnp.arange(B, dtype=jnp.int32)
    left_mask = (places[None, :] < left_dims[:, None]).astype(jnp.bfloat16)
    right_mask = (places[None, :] < right_dims[:, None]).astype(jnp.bfloat16)
    sector_of = (dest_owner[:, 0] * LSEC_DEV + left_slot).astype(jnp.int32)

    def per_block(block_index):
        current = psi[block_index].astype(jnp.float32)
        sector = sector_of[block_index]
        left_row = left_mask[sector]
        right_row = right_mask[block_index]
        summed = jnp.zeros((P_SIZE, B, B), jnp.float32)
        for channel in range(N_CHAN):
            right_kept = right_env[channel, block_index] * (right_row[:, None] * right_row[None, :])
            left_kept = left_env[channel, sector] * (left_row[:, None] * left_row[None, :])
            inner = jnp.einsum('pac,dc->pad', current, right_kept.astype(jnp.float32))
            mixed = jnp.einsum('sp,pad->sad', mpo[channel], inner, precision=lax.Precision.HIGHEST)
            mixed = lax.optimization_barrier(mixed.astype(jnp.bfloat16)).astype(jnp.float32)
            product = jnp.einsum('ea,sad->sed', left_kept.astype(jnp.float32), mixed)
            product = lax.optimization_barrier(product.astype(jnp.bfloat16)).astype(jnp.float32)
            summed = summed + product
        return summed.astype(jnp.bfloat16)

    return lax.map(per_block, jnp.arange(NB, dtype=jnp.int32))
```

```python
import functools

import jax
import jax.numpy as jnp
from jax import lax
from jax.experimental import pallas as pl
from jax.experimental.pallas import tpu as pltpu
from jax.sharding import PartitionSpec as P


def block_kernel(hi, rows, sector, right_dims, mpo, psi, left, own_right, *rest):
    other_rights = rest[: hi - 1]
    keep, send = rest[hi - 1 :]
    k = pl.program_id(0)
    states, width = psi.shape[1], psi.shape[2]
    stacked = left[0]
    parts = [
        jnp.dot(stacked, psi[0, p], preferred_element_type=jnp.float32) for p in range(states)
    ]
    r = right_dims[k]
    total = None
    for i in range(hi):
        right = own_right[0] if i == 0 else other_rights[i - 1][0]
        inside = (lax.broadcasted_iota(jnp.int32, right.shape, 0) < r) & (
            lax.broadcasted_iota(jnp.int32, right.shape, 1) < r
        )
        right = jnp.where(inside, right, jnp.zeros_like(right))
        mixed = []
        for s in range(states):
            acc = None
            for p in range(states):
                piece = parts[p][i * rows : (i + 1) * rows] * mpo[i, s * states + p]
                acc = piece if acc is None else acc + piece
            mixed.append(acc.astype(jnp.bfloat16))
        mixed = jnp.concatenate(mixed, axis=0)
        product = lax.dot_general(
            mixed, right, (((1,), (1,)), ((), ())), preferred_element_type=jnp.float32
        )
        total = product if total is None else total + product
    own = keep.shape[2]
    for s in range(states):
        keep[0, s] = total[s * rows : s * rows + own].astype(keep.dtype)
        send[0, :, s] = (
            total[s * rows + own : (s + 1) * rows].reshape(-1, own, width).astype(send.dtype)
        )


def blocks_call(first, count, hi, lo, own_rows, sector, right_dims, mpo, psi, left, own_right, others):
    states, width = psi.shape[1], psi.shape[2]
    rows = lo * own_rows
    grid_spec = pltpu.PrefetchScalarGridSpec(
        num_scalar_prefetch=3,
        grid=(count,),
        in_specs=[
            pl.BlockSpec((1, states, width, width), lambda k, sec, *_: (k + first, 0, 0, 0)),
            pl.BlockSpec((1, hi * rows, width), lambda k, sec, *_: (sec[k], 0, 0)),
            pl.BlockSpec((1, width, width), lambda k, *_: (k + first, 0, 0)),
        ]
        + [pl.BlockSpec((1, width, width), lambda k, *_: (k, 0, 0))] * (hi - 1),
        out_specs=[
            pl.BlockSpec((1, states, own_rows, width), lambda k, *_: (k, 0, 0, 0)),
            pl.BlockSpec((1, lo - 1, states, own_rows, width), lambda k, *_: (k, 0, 0, 0, 0)),
        ],
    )
    unit = states * width * width
    return pl.pallas_call(
        functools.partial(block_kernel, hi, rows),
        grid_spec=grid_spec,
        out_shape=[
            jax.ShapeDtypeStruct((count, states, own_rows, width), jnp.bfloat16),
            jax.ShapeDtypeStruct((count, lo - 1, states, own_rows, width), jnp.bfloat16),
        ],
        compiler_params=pltpu.CompilerParams(vmem_limit_bytes=48 * 2**20),
        cost_estimate=pl.CostEstimate(
            flops=count * 4 * hi * rows * unit,
            bytes_accessed=count * 5 * unit,
            transcendentals=0,
        ),
    )(sector, right_dims, mpo, psi, left, own_right, *others)


def on_device(n_chan, psi, mpo, left_env, right_env, left_dims, right_dims, dest_owner, left_slot):
    blocks, states, width = psi.shape[:3]
    sectors = left_env.shape[1]
    hi = 2 if n_chan % 2 == 0 else 1
    lo = n_chan // hi
    own_rows = width // n_chan
    here = lax.axis_index("chan")
    h, l = here // lo, here % lo

    def over_hi(x, i):
        pairs = [(c, ((c // lo + i) % hi) * lo + c % lo) for c in range(n_chan)]
        return lax.ppermute(x, "chan", pairs)

    def over_lo(x, j):
        pairs = [(c, (c // lo) * lo + (c % lo + j) % lo) for c in range(n_chan)]
        return lax.ppermute(x, "chan", pairs)

    chunks = 6 if blocks % 6 == 0 else 1
    count = blocks // chunks
    right = right_env[0]
    moved = []
    for m in range(chunks):
        piece = right[m * count : (m + 1) * count]
        if m >= 2:
            piece, _ = lax.optimization_barrier((piece, moved[m - 2]))
        moved.append([over_hi(piece, i) for i in range(1, hi)])

    places = jnp.arange(width, dtype=jnp.int32)
    left_mask = (places[None, :] < left_dims[:, None]).astype(jnp.bfloat16)
    left_kept = left_env[0] * (left_mask[:, :, None] * left_mask[:, None, :])
    left_kept = left_kept.reshape(sectors, hi, lo, own_rows, width)
    left_kept = jnp.take(left_kept, (l + jnp.arange(lo)) % lo, axis=2)

    def for_half(i):
        return lax.dynamic_index_in_dim(left_kept, (h + i) % hi, axis=1, keepdims=False)

    lefts = [for_half(0)] + [over_hi(for_half(i), i) for i in range(1, hi)]
    mpos = [mpo[0]] + [over_hi(mpo[0], i) for i in range(1, hi)]
    mpo_all = jnp.stack(mpos).reshape(hi, states * states)
    stacked = jnp.stack(lefts, axis=1).reshape(sectors, hi * lo * own_rows, width)
    every = lax.all_gather(stacked, "sec", axis=0, tiled=True)

    sector = dest_owner[:, 0] * sectors + left_slot
    outs = []
    for m in range(chunks):
        span = slice(m * count, (m + 1) * count)
        keep, send = blocks_call(
            m * count, count, hi, lo, own_rows, sector[span], right_dims[span], mpo_all,
            psi, every, right, moved[m],
        )
        total = keep.astype(jnp.float32)
        for j in range(1, lo):
            total = total + over_lo(send[:, j - 1], j).astype(jnp.float32)
        outs.append(total.astype(jnp.bfloat16))
    return jnp.concatenate(outs, axis=0)


def solution(mesh):
    in_specs = (
        P("sec", None, None, None),
        P("chan", None, None),
        P("chan", "sec", None, None),
        P("chan", "sec", None, None),
        P("sec"),
        P("sec"),
        P("sec", None),
        P("sec"),
    )
    out_specs = P("sec", None, "chan", None)
    return jax.shard_map(
        functools.partial(on_device, mesh.shape["chan"]),
        mesh=mesh,
        in_specs=in_specs,
        out_specs=out_specs,
        check_vma=False,
    )
```

```python
import functools

import jax
import jax.numpy as jnp
from jax import lax
from jax.experimental import pallas as pl
from jax.experimental.pallas import tpu as pltpu
from jax.sharding import PartitionSpec as P


def block_kernel(hi, rows, narrow, order, sector, right_dims, mpo, psi, *refs):
    lefts, rights = refs[:hi], refs[hi : 2 * hi]
    keep, send = refs[2 * hi :]
    states = psi.shape[1]
    stacked = jnp.concatenate([left[0] for left in lefts], axis=0)
    parts = [
        jnp.dot(stacked, psi[0, p], preferred_element_type=jnp.float32) for p in range(states)
    ]
    total = None
    for i in range(hi):
        right = rights[i][0]
        if not narrow:
            r = right_dims[order[pl.program_id(0)]]
            inside = (lax.broadcasted_iota(jnp.int32, right.shape, 0) < r) & (
                lax.broadcasted_iota(jnp.int32, right.shape, 1) < r
            )
            right = jnp.where(inside, right, jnp.zeros_like(right))
        mixed = []
        for s in range(states):
            acc = None
            for p in range(states):
                piece = parts[p][i * rows : (i + 1) * rows] * mpo[i, s * states + p]
                acc = piece if acc is None else acc + piece
            mixed.append(acc.astype(jnp.bfloat16))
        mixed = jnp.concatenate(mixed, axis=0)
        product = lax.dot_general(
            mixed, right, (((1,), (1,)), ((), ())), preferred_element_type=jnp.float32
        )
        total = product if total is None else total + product
    own = keep.shape[2]
    for s in range(states):
        keep[0, s] = total[s * rows : s * rows + own].astype(keep.dtype)
        for j in range(send.shape[1]):
            at = s * rows + (j + 1) * own
            send[0, j, s] = total[at : at + own].astype(send.dtype)


def blocks_call(hi, lo, own_rows, narrow, order, sector, right_dims, mpo, psi, lefts, right, others):
    states, width = psi.shape[1], psi.shape[2]
    count = order.shape[0]
    across = width // 2 if narrow else width
    rows = lo * own_rows

    def by_block(k, order, sector, *_):
        return (order[k], 0, 0)

    def by_sector(k, order, sector, *_):
        return (sector[order[k]], 0, 0)

    grid_spec = pltpu.PrefetchScalarGridSpec(
        num_scalar_prefetch=4,
        grid=(count,),
        in_specs=[
            pl.BlockSpec((1, states, width, across), lambda *at: by_block(*at) + (0,)),
        ]
        + [pl.BlockSpec((1, rows, width), by_sector)] * hi
        + [pl.BlockSpec((1, across, across), by_block)]
        + [pl.BlockSpec((1, across, across), lambda k, *_: (k, 0, 0))] * (hi - 1),
        out_specs=[
            pl.BlockSpec((1, states, own_rows, across), lambda k, *_: (k, 0, 0, 0)),
            pl.BlockSpec((1, lo - 1, states, own_rows, across), lambda k, *_: (k, 0, 0, 0, 0)),
        ],
    )
    return pl.pallas_call(
        functools.partial(block_kernel, hi, rows, narrow),
        grid_spec=grid_spec,
        out_shape=[
            jax.ShapeDtypeStruct((count, states, own_rows, across), jnp.bfloat16),
            jax.ShapeDtypeStruct((count, lo - 1, states, own_rows, across), jnp.bfloat16),
        ],
        compiler_params=pltpu.CompilerParams(vmem_limit_bytes=48 * 2**20),
        cost_estimate=pl.CostEstimate(
            flops=count * 2 * hi * rows * states * across * (width + across),
            bytes_accessed=count * 5 * states * width * across,
            transcendentals=0,
        ),
    )(order, sector, right_dims, mpo, psi, *lefts, right, *others)


def add_kernel(terms, order, *refs):
    out = refs[-1]
    total = refs[0][0].astype(jnp.float32)
    for j in range(1, terms):
        total = total + refs[j][0].astype(jnp.float32)
    across = total.shape[-1]
    out[0, :, :, :across] = total.astype(out.dtype)
    if across < out.shape[-1]:
        out[0, :, :, across:] = jnp.zeros(out.shape[1:3] + (out.shape[-1] - across,), out.dtype)


def add_call(shape, order, terms, out):
    block = pl.BlockSpec((1,) + terms[0].shape[1:], lambda k, order: (k, 0, 0, 0))
    grid_spec = pltpu.PrefetchScalarGridSpec(
        num_scalar_prefetch=1,
        grid=(order.shape[0],),
        in_specs=[block] * len(terms) + ([] if out is None else [pl.BlockSpec(memory_space=pl.ANY)]),
        out_specs=pl.BlockSpec((1,) + shape[1:], lambda k, order: (order[k], 0, 0, 0)),
    )
    return pl.pallas_call(
        functools.partial(add_kernel, len(terms)),
        grid_spec=grid_spec,
        out_shape=jax.ShapeDtypeStruct(shape, jnp.bfloat16),
        input_output_aliases={} if out is None else {1 + len(terms): 0},
        compiler_params=pltpu.CompilerParams(vmem_limit_bytes=32 * 2**20),
        cost_estimate=pl.CostEstimate(
            flops=terms[0].size, bytes_accessed=6 * terms[0].size, transcendentals=0
        ),
    )(order, *terms, *([] if out is None else [out]))


def after(x, *others):
    return lax.optimization_barrier((x, others))[0]


def on_device(n_chan, psi, mpo, left_env, right_env, left_dims, right_dims, dest_owner, left_slot):
    blocks, states, width = psi.shape[:3]
    sectors = left_env.shape[1]
    half = width // 2
    hi = 2 if n_chan % 2 == 0 else 1
    lo = n_chan // hi
    own_rows = width // n_chan
    here = lax.axis_index("chan")
    h, l = here // lo, here % lo
    right = right_env[0]

    def over_hi(x, i):
        pairs = [(c, ((c // lo + i) % hi) * lo + c % lo) for c in range(n_chan)]
        return lax.ppermute(x, "chan", pairs)

    def over_lo(x, j):
        pairs = [(c, (c // lo) * lo + (c % lo + j) % lo) for c in range(n_chan)]
        return lax.ppermute(x, "chan", pairs)

    def to_partners(x):
        return [over_hi(x, i) for i in range(1, hi)]

    wide = right_dims > half
    n_wide = jnp.sum(wide.astype(jnp.int32))
    most_wide = lax.pmax(n_wide, "sec")
    ids = jnp.arange(blocks, dtype=jnp.int32)
    before = ids[None, :] < ids[:, None]
    ahead = jnp.sum((before & (wide[None, :] == wide[:, None])).astype(jnp.int32), axis=1)
    place = jnp.where(wide, ahead, n_wide + ahead)
    order = jnp.sum(jnp.where(place[None, :] == ids[:, None], ids[None, :], 0), axis=1)
    sector = dest_owner[:, 0] * sectors + left_slot

    step = max(blocks // 6, 1)

    def wide_piece(span):
        return jnp.take(right, order[span], axis=0, mode="clip")

    def narrow_piece(span):
        return jnp.take(right[:, :half, :half], order[span], axis=0, mode="clip")

    left_mask = (jnp.arange(width, dtype=jnp.int32)[None, :] < left_dims[:, None]).astype(jnp.bfloat16)
    left_kept = left_env[0] * (left_mask[:, :, None] * left_mask[:, None, :])
    left_kept = left_kept.reshape(sectors, hi, lo, own_rows, width)
    left_kept = jnp.take(left_kept, (l + jnp.arange(lo)) % lo, axis=2)

    def for_half(i):
        picked = lax.dynamic_index_in_dim(left_kept, (h + i) % hi, axis=1, keepdims=False)
        return picked.reshape(sectors, lo * own_rows, width)

    shards = [for_half(0)] + [over_hi(for_half(i), i) for i in range(1, hi)]
    mpos = [mpo[0]] + to_partners(mpo[0])
    mpo_all = jnp.stack(mpos).reshape(hi, states * states)
    lefts = []
    for shard in shards:
        if lefts:
            shard = after(shard, lefts[-1])
        else:
            shard = after(shard, most_wide)
        lefts.append(lax.all_gather(shard, "sec", axis=0, tiled=True))

    early = [slice(0, step), slice(step, 2 * step)]
    moved = [to_partners(wide_piece(span)) for span in early]

    def run(cap, order, moved, lefts, mpo_all):
        spans = [(slice(a, min(a + step, cap)), False) for a in range(0, cap, step)]
        rest = blocks - cap
        pieces = -(-rest // max(step + 1, 1))
        for q in range(pieces):
            a, b = cap + rest * q // pieces, cap + rest * (q + 1) // pieces
            spans.append((slice(a, b), True))
        moved = list(moved)
        keeps, sends = [], []

        def compute(m):
            span, narrow = spans[m]
            keep, send = blocks_call(
                hi, lo, own_rows, narrow, order[span], sector, right_dims, mpo_all,
                psi, lefts, right, moved[m],
            )
            keeps.append(keep)
            sends.append(send)

        for m in range(len(moved), len(spans)):
            span, narrow = spans[m]
            piece = narrow_piece(span) if narrow else wide_piece(span)
            if m - 3 >= 0:
                compute(m - 3)
                piece = after(piece, moved[m - 2], sends[m - 3])
            moved.append(to_partners(piece))
        for m in range(len(sends), len(spans)):
            compute(m)
        out = None
        for m, (span, narrow) in enumerate(spans):
            arrived = [over_lo(sends[m][:, j - 1], j) for j in range(1, lo)]
            terms = [after(keeps[m], sends[min(m + 2, len(spans) - 1)])] + arrived
            out = add_call((blocks, states, own_rows, width), order[span], terms, out)
        return out

    caps = sorted({max(2 * step, blocks * q // 12) for q in (7, 8, 9)} | {blocks})
    which = sum((most_wide > cap).astype(jnp.int32) for cap in caps[:-1])
    return lax.switch(
        which, [functools.partial(run, cap) for cap in caps], order, moved, lefts, mpo_all
    )


def solution(mesh):
    in_specs = (
        P("sec", None, None, None),
        P("chan", None, None),
        P("chan", "sec", None, None),
        P("chan", "sec", None, None),
        P("sec"),
        P("sec"),
        P("sec", None),
        P("sec"),
    )
    out_specs = P("sec", None, "chan", None)
    return jax.shard_map(
        functools.partial(on_device, mesh.shape["chan"]),
        mesh=mesh,
        in_specs=in_specs,
        out_specs=out_specs,
        check_vma=False,
    )
```

```python
import functools

import jax
import jax.numpy as jnp
from jax import lax
from jax.experimental import pallas as pl
from jax.experimental.pallas import tpu as pltpu
from jax.sharding import PartitionSpec as P

ANY = pl.BlockSpec(memory_space=pl.ANY)
SMEM = pl.BlockSpec(memory_space=pltpu.SMEM)


def after(x, *others):
    return lax.optimization_barrier((x, others))[0]


def left_kernel(hi, lo, here, dims, left, *outs):
    own = outs[0].shape[1] // lo
    h, l = here[0] // lo, here[0] % lo
    r = dims[pl.program_id(0)]
    for i in range(hi):
        for j in range(lo):
            start = pl.multiple_of((((h + i) % hi) * lo + (l + j) % lo) * own, own)
            piece = left[0, pl.ds(start, own), :]
            inside = (lax.broadcasted_iota(jnp.int32, piece.shape, 0) + start < r) & (
                lax.broadcasted_iota(jnp.int32, piece.shape, 1) < r
            )
            outs[i][0, j * own : (j + 1) * own] = jnp.where(inside, piece, jnp.zeros_like(piece))


def left_call(hi, lo, own_rows, here, dims, left):
    sectors, width = left.shape[:2]
    block = (1, lo * own_rows, width)
    return pl.pallas_call(
        functools.partial(left_kernel, hi, lo),
        grid_spec=pltpu.PrefetchScalarGridSpec(
            num_scalar_prefetch=2,
            grid=(sectors,),
            in_specs=[pl.BlockSpec((1, width, width), lambda s, *_: (s, 0, 0))],
            out_specs=[pl.BlockSpec(block, lambda s, *_: (s, 0, 0))] * hi,
        ),
        out_shape=[jax.ShapeDtypeStruct((sectors,) + block[1:], left.dtype)] * hi,
        compiler_params=pltpu.CompilerParams(vmem_limit_bytes=32 * 2**20),
        cost_estimate=pl.CostEstimate(flops=left.size, bytes_accessed=4 * left.size, transcendentals=0),
    )(here, dims, left)


def copy_pieces(order, right, pieces, spans, sems):
    copies = []
    for piece, span in zip(pieces, spans):
        across = piece.shape[-1]
        for n, at in enumerate(range(span.start, span.stop)):
            source = right.at[order[at]]
            if across < right.shape[-1]:
                source = right.at[order[at], pl.ds(0, across), pl.ds(0, across)]
            copies.append(pltpu.make_async_copy(source, piece.at[n], sems.at[len(copies)]))
    for copy in copies:
        copy.start()
    for copy in copies:
        copy.wait()


def plan_kernel(spans, dims, right, order, count, *refs):
    pieces, sems = refs[:-1], refs[-1]
    blocks, half = dims.shape[0], right.shape[-1] // 2

    def place(keep_wide):
        def body(k, at):
            mine = (dims[k] > half) == keep_wide

            @pl.when(mine)
            def _():
                order[at] = k

            return at + mine.astype(jnp.int32)

        return body

    wide = lax.fori_loop(0, blocks, place(True), jnp.int32(0))
    count[0] = wide
    lax.fori_loop(0, blocks, place(False), wide)
    copy_pieces(order, right, pieces, spans, sems)


def plan_call(spans, dims, right):
    width = right.shape[-1]
    total = sum(span.stop - span.start for span in spans)
    return pl.pallas_call(
        functools.partial(plan_kernel, spans),
        in_specs=[SMEM, ANY],
        out_specs=[SMEM, SMEM] + [ANY] * len(spans),
        out_shape=[jax.ShapeDtypeStruct(dims.shape, jnp.int32), jax.ShapeDtypeStruct((1,), jnp.int32)]
        + [jax.ShapeDtypeStruct((s.stop - s.start, width, width), right.dtype) for s in spans],
        scratch_shapes=[pltpu.SemaphoreType.DMA((total,))],
        cost_estimate=pl.CostEstimate(flops=0, bytes_accessed=4 * total * width * width, transcendentals=0),
    )(dims, right)


def pack_kernel(spans, order, right, *refs):
    copy_pieces(order, right, refs[:-1], spans, refs[-1])


def pack_call(spans, widths, order, right):
    total = sum(span.stop - span.start for span in spans)
    shapes = [jax.ShapeDtypeStruct((s.stop - s.start, w, w), right.dtype) for s, w in zip(spans, widths)]
    return pl.pallas_call(
        functools.partial(pack_kernel, spans),
        in_specs=[SMEM, ANY],
        out_specs=[ANY] * len(spans),
        out_shape=shapes,
        scratch_shapes=[pltpu.SemaphoreType.DMA((total,))],
        cost_estimate=pl.CostEstimate(
            flops=0, bytes_accessed=4 * sum(s.size for s in shapes), transcendentals=0
        ),
    )(order, right)


def pick_kernel(hi, order, near, row, *refs):
    sources, (*outs, sems) = refs[: 2 * hi], refs[2 * hi :]
    blocks = order.shape[0]

    def start(n, _):
        k = order[n]
        for i in range(hi):
            for far in range(2):

                @pl.when(near[k] == 1 - far)
                def _():
                    pltpu.make_async_copy(
                        sources[2 * i + far].at[row[k]], outs[i].at[n], sems.at[i, n]
                    ).start()

        return 0

    def finish(n, _):
        for i in range(hi):
            pltpu.make_async_copy(sources[2 * i].at[0], outs[i].at[n], sems.at[i, n]).wait()
        return 0

    lax.fori_loop(0, blocks, start, 0)
    lax.fori_loop(0, blocks, finish, 0)


def pick_call(hi, order, near, row, sources):
    blocks = order.shape[0]
    shape = (blocks,) + sources[0].shape[1:]
    return pl.pallas_call(
        functools.partial(pick_kernel, hi),
        in_specs=[SMEM] * 3 + [ANY] * (2 * hi),
        out_specs=[ANY] * hi,
        out_shape=[jax.ShapeDtypeStruct(shape, sources[0].dtype)] * hi,
        scratch_shapes=[pltpu.SemaphoreType.DMA((hi, blocks))],
        cost_estimate=pl.CostEstimate(
            flops=0, bytes_accessed=4 * hi * blocks * shape[1] * shape[2], transcendentals=0
        ),
    )(order, near, row, *sources)


def block_kernel(hi, rows, narrow, first, order, right_dims, mpo, psi, *refs):
    lefts, rights = refs[:hi], refs[hi : 2 * hi]
    keep, send = refs[2 * hi :]
    states = psi.shape[1]
    stacked = jnp.concatenate([left[0] for left in lefts], axis=0)
    parts = [
        jnp.dot(stacked, psi[0, p], preferred_element_type=jnp.float32) for p in range(states)
    ]
    total = None
    for i in range(hi):
        right = rights[i][0]
        if not narrow:
            r = right_dims[order[pl.program_id(0) + first]]
            inside = (lax.broadcasted_iota(jnp.int32, right.shape, 0) < r) & (
                lax.broadcasted_iota(jnp.int32, right.shape, 1) < r
            )
            right = jnp.where(inside, right, jnp.zeros_like(right))
        mixed = []
        for s in range(states):
            acc = None
            for p in range(states):
                piece = parts[p][i * rows : (i + 1) * rows] * mpo[i, s * states + p]
                acc = piece if acc is None else acc + piece
            mixed.append(acc.astype(jnp.bfloat16))
        mixed = jnp.concatenate(mixed, axis=0)
        product = lax.dot_general(
            mixed, right, (((1,), (1,)), ((), ())), preferred_element_type=jnp.float32
        )
        total = product if total is None else total + product
    own = keep.shape[2]
    for s in range(states):
        keep[0, s] = total[s * rows : s * rows + own].astype(keep.dtype)
        for j in range(send.shape[0]):
            at = s * rows + (j + 1) * own
            send[j, 0, s] = total[at : at + own].astype(send.dtype)


def blocks_call(hi, lo, own_rows, narrow, span, order, right_dims, mpo, psi, lefts, right, others):
    states, width = psi.shape[1], psi.shape[2]
    first, count = span.start, span.stop - span.start
    across = width // 2 if narrow else width
    rows = lo * own_rows

    def by_block(k, order, *_):
        return (order[k + first], 0, 0)

    grid_spec = pltpu.PrefetchScalarGridSpec(
        num_scalar_prefetch=3,
        grid=(count,),
        in_specs=[
            pl.BlockSpec((1, states, width, across), lambda *at: by_block(*at) + (0,)),
        ]
        + [pl.BlockSpec((1, rows, width), lambda k, *_: (k + first, 0, 0))] * hi
        + [pl.BlockSpec((1, across, across), by_block)]
        + [pl.BlockSpec((1, across, across), lambda k, *_: (k, 0, 0))] * (hi - 1),
        out_specs=[
            pl.BlockSpec((1, states, own_rows, across), lambda k, *_: (k, 0, 0, 0)),
            pl.BlockSpec((lo - 1, 1, states, own_rows, across), lambda k, *_: (0, k, 0, 0, 0)),
        ],
    )
    return pl.pallas_call(
        functools.partial(block_kernel, hi, rows, narrow, first),
        grid_spec=grid_spec,
        out_shape=[
            jax.ShapeDtypeStruct((count, states, own_rows, across), jnp.bfloat16),
            jax.ShapeDtypeStruct((lo - 1, count, states, own_rows, across), jnp.bfloat16),
        ],
        compiler_params=pltpu.CompilerParams(vmem_limit_bytes=40 * 2**20),
        cost_estimate=pl.CostEstimate(
            flops=count * 2 * hi * rows * states * across * (width + across),
            bytes_accessed=count * 5 * states * width * across,
            transcendentals=0,
        ),
    )(order, right_dims, mpo, psi, *lefts, right, *others)


def add_kernel(terms, span, order, *refs):
    out, total, sems = refs[-3:]
    across = refs[0].shape[-1]
    copies = []
    for k in range(span.stop - span.start):
        acc = refs[0][k].astype(jnp.float32)
        for j in range(1, terms):
            acc = acc + refs[j][k].astype(jnp.float32)
        total[k, :, :, :across] = acc.astype(total.dtype)
        if across < total.shape[-1]:
            total[k, :, :, across:] = jnp.zeros(acc.shape[:-1] + (total.shape[-1] - across,), total.dtype)
        copy = pltpu.make_async_copy(total.at[k], out.at[order[k + span.start]], sems.at[k])
        copy.start()
        copies.append(copy)
    for copy in copies:
        copy.wait()


def add_call(shape, span, order, terms, out):
    count = span.stop - span.start
    return pl.pallas_call(
        functools.partial(add_kernel, len(terms), span),
        in_specs=[SMEM]
        + [pl.BlockSpec(memory_space=pltpu.VMEM)] * len(terms)
        + ([] if out is None else [ANY]),
        out_specs=ANY,
        out_shape=jax.ShapeDtypeStruct(shape, jnp.bfloat16),
        scratch_shapes=[
            pltpu.VMEM((count,) + shape[1:], jnp.bfloat16),
            pltpu.SemaphoreType.DMA((count,)),
        ],
        input_output_aliases={} if out is None else {1 + len(terms): 0},
        compiler_params=pltpu.CompilerParams(vmem_limit_bytes=24 * 2**20),
        cost_estimate=pl.CostEstimate(
            flops=terms[0].size, bytes_accessed=6 * terms[0].size, transcendentals=0
        ),
    )(order, *terms, *([] if out is None else [out]))


def on_device(n_chan, n_sec, psi, mpo, left_env, right_env, left_dims, right_dims, dest_owner, left_slot):
    blocks, states, width = psi.shape[:3]
    sectors = left_env.shape[1]
    half = width // 2
    hi = 2 if n_chan % 2 == 0 else 1
    lo = n_chan // hi
    own_rows = width // n_chan
    here, me = lax.axis_index("chan"), lax.axis_index("sec")
    right = right_env[0]
    step = max(blocks // 6, 1)

    def over_hi(x, i):
        pairs = [(c, ((c // lo + i) % hi) * lo + c % lo) for c in range(n_chan)]
        return lax.ppermute(x, "chan", pairs)

    def over_lo(x, j):
        pairs = [(c, (c // lo) * lo + (c % lo + j) % lo) for c in range(n_chan)]
        return lax.ppermute(x, "chan", pairs)

    def over_bit(x, bit):
        return lax.ppermute(x, "sec", [(i, i ^ bit) for i in range(n_sec)])

    def to_partners(x):
        return [over_hi(x, i) for i in range(1, hi)]

    shards = left_call(hi, lo, own_rows, here[None], left_dims, left_env[0])
    early = [slice(m * step, (m + 1) * step) for m in range(3)]
    order, n_wide, *pieces = plan_call(early, right_dims, right)

    bits = [1 << b for b in range(1, n_sec.bit_length() - 1)]
    cut = sectors // 2

    def swap(i):
        if i == 0:
            return [shards[0][:cut], shards[0][cut:]]
        return [over_hi(shards[i][:cut], i), over_hi(shards[i][cut:], i)]

    def spread(parts):
        first, second = parts
        for bit, other in zip(bits, bits[::-1]):
            first = jnp.concatenate([first, over_bit(first, bit)])
            second = jnp.concatenate([second, over_bit(second, other)])
        near = jnp.concatenate([first, second])
        return [near, over_bit(near, 1)]

    gap = dest_owner[:, 0] ^ me
    up = sum(((gap // bit) % 2) << t for t, bit in enumerate(bits))
    down = sum(((gap // bit) % 2) << t for t, bit in enumerate(bits[::-1]))
    near = 1 - gap % 2
    row = jnp.where(
        left_slot < cut,
        up * cut + left_slot,
        (n_sec // 2) * cut + down * (sectors - cut) + left_slot - cut,
    )

    swapped = [swap(i) for i in range(hi)]
    mpo_all = jnp.stack([mpo[0]] + to_partners(mpo[0])).reshape(hi, states * states)
    sources = []
    for parts in swapped:
        sources += spread(parts)
    moved = [to_partners(after(pieces[0], swapped[-1][0]))]
    moved.append(to_partners(after(pieces[1], swapped[-1][1])))
    most_wide = lax.pmax(after(n_wide, moved[0]), "sec")[0]
    lefts = pick_call(hi, order, near, row, sources)

    def compute(span, narrow, order, lefts, mpo_all, others):
        return blocks_call(
            hi, lo, own_rows, narrow, span, order, right_dims, mpo_all, psi, lefts, right, others
        )

    def exchange(send):
        return [over_lo(send[j - 1], j) for j in range(1, lo)]

    keep, send = compute(early[0], False, order, lefts, mpo_all, moved[0])
    terms = [keep] + exchange(send)

    def run(cap, order, moved, third, lefts, mpo_all, terms):
        spans = [(slice(a, min(a + step, cap)), False) for a in range(0, cap, step)]
        rest = blocks - cap
        count = -(-rest // (step + 1))
        for q in range(count):
            a, b = cap + rest * q // count, cap + rest * (q + 1) // count
            spans.append((slice(a, b), True))
        total = len(spans)
        moved = list(moved)
        moved.append(to_partners(third))
        later = spans[3:]
        pieces = [third] * 3
        pieces += pack_call(
            [s for s, _ in later], [half if n else width for _, n in later], order, right
        )
        shape = (blocks, states, own_rows, width)
        terms = [terms]
        out = add_call(shape, spans[0][0], order, terms[0], None)
        added = 1
        for m in range(1, total):
            while added < m - 2:
                out = add_call(shape, spans[added][0], order, terms[added], out)
                added += 1
            mpo_now, out = lax.optimization_barrier((mpo_all, out))
            if m + 2 < total:
                waits = (moved[m], terms[m - 1][0]) if m > 1 else ()
                moved.append(to_partners(after(pieces[m + 2], waits)))
            keep, send = compute(*spans[m], order, lefts, mpo_now, moved[m])
            terms.append([keep] + exchange(send))
        for m in range(added, total):
            out = add_call(shape, spans[m][0], order, terms[m], out)
        return out

    caps = sorted({max(3 * step, blocks * q // 12) for q in (7, 8, 9)} | {blocks})
    which = sum((most_wide > cap).astype(jnp.int32) for cap in caps[:-1])
    return lax.switch(
        which,
        [functools.partial(run, cap) for cap in caps],
        order, moved, pieces[2], lefts, mpo_all, terms,
    )


def solution(mesh):
    in_specs = (
        P("sec", None, None, None),
        P("chan", None, None),
        P("chan", "sec", None, None),
        P("chan", "sec", None, None),
        P("sec"),
        P("sec"),
        P("sec", None),
        P("sec"),
    )
    out_specs = P("sec", None, "chan", None)
    return jax.shard_map(
        functools.partial(on_device, mesh.shape["chan"], mesh.shape["sec"]),
        mesh=mesh,
        in_specs=in_specs,
        out_specs=out_specs,
        check_vma=False,
    )
```

```python
import functools

import jax
import jax.numpy as jnp
from jax import lax
from jax.experimental import pallas as pl
from jax.experimental.pallas import tpu as pltpu
from jax.sharding import PartitionSpec as P

ANY = pl.BlockSpec(memory_space=pl.ANY)
SMEM = pl.BlockSpec(memory_space=pltpu.SMEM)


def after(x, *others):
    return lax.optimization_barrier((x, others))[0]


def left_kernel(hi, lo, here, dims, left, *outs):
    own = outs[0].shape[1] // lo
    h, l = here[0] // lo, here[0] % lo
    r = dims[pl.program_id(0)]
    for i in range(hi):
        for j in range(lo):
            start = pl.multiple_of((((h + i) % hi) * lo + (l + j) % lo) * own, own)
            piece = left[0, pl.ds(start, own), :]
            inside = (lax.broadcasted_iota(jnp.int32, piece.shape, 0) + start < r) & (
                lax.broadcasted_iota(jnp.int32, piece.shape, 1) < r
            )
            outs[i][0, j * own : (j + 1) * own] = jnp.where(inside, piece, jnp.zeros_like(piece))


def left_call(hi, lo, own_rows, here, dims, left):
    sectors, width = left.shape[:2]
    block = (1, lo * own_rows, width)
    return pl.pallas_call(
        functools.partial(left_kernel, hi, lo),
        grid_spec=pltpu.PrefetchScalarGridSpec(
            num_scalar_prefetch=2,
            grid=(sectors,),
            in_specs=[pl.BlockSpec((1, width, width), lambda s, *_: (s, 0, 0))],
            out_specs=[pl.BlockSpec(block, lambda s, *_: (s, 0, 0))] * hi,
        ),
        out_shape=[jax.ShapeDtypeStruct((sectors,) + block[1:], left.dtype)] * hi,
        compiler_params=pltpu.CompilerParams(vmem_limit_bytes=32 * 2**20),
        cost_estimate=pl.CostEstimate(flops=left.size, bytes_accessed=4 * left.size, transcendentals=0),
    )(here, dims, left)


def copy_pieces(order, right, pieces, spans, sems):
    copies = []
    for piece, span in zip(pieces, spans):
        across = piece.shape[-1]
        for n, at in enumerate(range(span.start, span.stop)):
            source = right.at[order[at]]
            if across < right.shape[-1]:
                source = right.at[order[at], pl.ds(0, across), pl.ds(0, across)]
            copies.append(pltpu.make_async_copy(source, piece.at[n], sems.at[len(copies)]))
    for copy in copies:
        copy.start()
    for copy in copies:
        copy.wait()


def plan_kernel(spans, dims, right, order, count, *refs):
    pieces, sems = refs[:-1], refs[-1]
    blocks, half = dims.shape[0], right.shape[-1] // 2

    def place(keep_wide):
        def body(k, at):
            mine = (dims[k] > half) == keep_wide

            @pl.when(mine)
            def _():
                order[at] = k

            return at + mine.astype(jnp.int32)

        return body

    wide = lax.fori_loop(0, blocks, place(True), jnp.int32(0))
    count[0] = wide
    lax.fori_loop(0, blocks, place(False), wide)
    copy_pieces(order, right, pieces, spans, sems)


def plan_call(spans, dims, right):
    width = right.shape[-1]
    total = sum(span.stop - span.start for span in spans)
    return pl.pallas_call(
        functools.partial(plan_kernel, spans),
        in_specs=[SMEM, ANY],
        out_specs=[SMEM, SMEM] + [ANY] * len(spans),
        out_shape=[jax.ShapeDtypeStruct(dims.shape, jnp.int32), jax.ShapeDtypeStruct((1,), jnp.int32)]
        + [jax.ShapeDtypeStruct((s.stop - s.start, width, width), right.dtype) for s in spans],
        scratch_shapes=[pltpu.SemaphoreType.DMA((total,))],
        cost_estimate=pl.CostEstimate(flops=0, bytes_accessed=4 * total * width * width, transcendentals=0),
    )(dims, right)


def block_kernel(hi, rows, narrow, first, order, right_dims, is_near, row, sector, mpo, psi, *refs):
    lefts, rights = refs[: 2 * hi - 1], refs[2 * hi - 1 : 3 * hi - 1]
    keep, send = refs[3 * hi - 1 :]
    states = psi.shape[1]
    k = order[pl.program_id(0) + first]
    by_self = jnp.full(lefts[0].shape[1:], is_near[k], jnp.int32) > 0
    stacked = jnp.concatenate(
        [lefts[0][0]]
        + [jnp.where(by_self, lefts[2 * i - 1][0], lefts[2 * i][0]) for i in range(1, hi)],
        axis=0,
    )
    parts = [
        jnp.dot(stacked, psi[0, p], preferred_element_type=jnp.float32) for p in range(states)
    ]
    total = None
    for i in range(hi):
        right = rights[i][0]
        if not narrow:
            r = right_dims[k]
            inside = (lax.broadcasted_iota(jnp.int32, right.shape, 0) < r) & (
                lax.broadcasted_iota(jnp.int32, right.shape, 1) < r
            )
            right = jnp.where(inside, right, jnp.zeros_like(right))
        mixed = []
        for s in range(states):
            acc = None
            for p in range(states):
                piece = parts[p][i * rows : (i + 1) * rows] * mpo[i, s * states + p]
                acc = piece if acc is None else acc + piece
            mixed.append(acc.astype(jnp.bfloat16))
        mixed = jnp.concatenate(mixed, axis=0)
        product = lax.dot_general(
            mixed, right, (((1,), (1,)), ((), ())), preferred_element_type=jnp.float32
        )
        total = product if total is None else total + product
    own = keep.shape[2]
    for s in range(states):
        keep[0, s] = total[s * rows : s * rows + own].astype(keep.dtype)
        for j in range(send.shape[0]):
            at = s * rows + (j + 1) * own
            send[j, 0, s] = total[at : at + own].astype(send.dtype)


def blocks_call(hi, lo, own_rows, narrow, span, scalars, mpo, psi, lefts, right, others):
    states, width = psi.shape[1], psi.shape[2]
    first, count = span.start, span.stop - span.start
    across = width // 2 if narrow else width
    rows = lo * own_rows

    def by_block(k, order, *_):
        return (order[k + first], 0, 0)

    def by_sector(k, order, right_dims, is_near, row, sector, *_):
        return (sector[order[k + first]], 0, 0)

    def by_row(far):
        def index(k, order, right_dims, is_near, row, *_):
            block = order[k + first]
            return (jnp.where(is_near[block] == 1 - far, row[block], 0), 0, 0)

        return index

    grid_spec = pltpu.PrefetchScalarGridSpec(
        num_scalar_prefetch=6,
        grid=(count,),
        in_specs=[
            pl.BlockSpec((1, states, width, across), lambda *at: by_block(*at) + (0,)),
        ]
        + [pl.BlockSpec((1, rows, width), by_sector)]
        + [pl.BlockSpec((1, rows, width), by_row(far)) for _ in range(hi - 1) for far in range(2)]
        + [pl.BlockSpec((1, across, across), by_block)]
        + [pl.BlockSpec((1, across, across), lambda k, *_: (k, 0, 0))] * (hi - 1),
        out_specs=[
            pl.BlockSpec((1, states, own_rows, across), lambda k, *_: (k, 0, 0, 0)),
            pl.BlockSpec((lo - 1, 1, states, own_rows, across), lambda k, *_: (0, k, 0, 0, 0)),
        ],
    )
    return pl.pallas_call(
        functools.partial(block_kernel, hi, rows, narrow, first),
        grid_spec=grid_spec,
        out_shape=[
            jax.ShapeDtypeStruct((count, states, own_rows, across), jnp.bfloat16),
            jax.ShapeDtypeStruct((lo - 1, count, states, own_rows, across), jnp.bfloat16),
        ],
        compiler_params=pltpu.CompilerParams(vmem_limit_bytes=40 * 2**20),
        cost_estimate=pl.CostEstimate(
            flops=count * 2 * hi * rows * states * across * (width + across),
            bytes_accessed=count * 5 * states * width * across,
            transcendentals=0,
        ),
    )(*scalars, mpo, psi, *lefts, right, *others)


def add_kernel(terms, span, order, *refs):
    out, total, sems = refs[-3:]
    across = refs[0].shape[-1]
    copies = []
    for k in range(span.stop - span.start):
        acc = refs[0][k].astype(jnp.float32)
        for j in range(1, terms):
            acc = acc + refs[j][k].astype(jnp.float32)
        total[k, :, :, :across] = acc.astype(total.dtype)
        if across < total.shape[-1]:
            total[k, :, :, across:] = jnp.zeros(acc.shape[:-1] + (total.shape[-1] - across,), total.dtype)
        copy = pltpu.make_async_copy(total.at[k], out.at[order[k + span.start]], sems.at[k])
        copy.start()
        copies.append(copy)
    for copy in copies:
        copy.wait()


def add_call(shape, span, order, terms, out):
    count = span.stop - span.start
    return pl.pallas_call(
        functools.partial(add_kernel, len(terms), span),
        in_specs=[SMEM]
        + [pl.BlockSpec(memory_space=pltpu.VMEM)] * len(terms)
        + ([] if out is None else [ANY]),
        out_specs=ANY,
        out_shape=jax.ShapeDtypeStruct(shape, jnp.bfloat16),
        scratch_shapes=[
            pltpu.VMEM((count,) + shape[1:], jnp.bfloat16),
            pltpu.SemaphoreType.DMA((count,)),
        ],
        input_output_aliases={} if out is None else {1 + len(terms): 0},
        compiler_params=pltpu.CompilerParams(vmem_limit_bytes=24 * 2**20),
        cost_estimate=pl.CostEstimate(
            flops=terms[0].size, bytes_accessed=6 * terms[0].size, transcendentals=0
        ),
    )(order, *terms, *([] if out is None else [out]))


def on_device(n_chan, n_sec, psi, mpo, left_env, right_env, left_dims, right_dims, dest_owner, left_slot):
    blocks, states, width = psi.shape[:3]
    sectors = left_env.shape[1]
    half = width // 2
    hi = 2 if n_chan % 2 == 0 else 1
    lo = n_chan // hi
    own_rows = width // n_chan
    here, me = lax.axis_index("chan"), lax.axis_index("sec")
    right = right_env[0]
    step = max(blocks // 6, 1)

    def over_hi(x, i):
        pairs = [(c, ((c // lo + i) % hi) * lo + c % lo) for c in range(n_chan)]
        return lax.ppermute(x, "chan", pairs)

    def over_lo(x, j):
        pairs = [(c, (c // lo) * lo + (c % lo + j) % lo) for c in range(n_chan)]
        return lax.ppermute(x, "chan", pairs)

    def over_bit(x, bit):
        return lax.ppermute(x, "sec", [(i, i ^ bit) for i in range(n_sec)])

    def to_partners(x):
        return [over_hi(x, i) for i in range(1, hi)]

    pair = max(step // 2, 1)
    early = [slice(0, pair), slice(pair, step), slice(step, 2 * step), slice(2 * step, 3 * step)]
    fixed = early[-1].stop
    order, n_wide, *pieces = plan_call(early + [slice(fixed, blocks)], right_dims, right)
    mpo_now, dims_now = lax.optimization_barrier((mpo[0], left_dims, n_wide))[:2]
    mpo_all = jnp.stack([mpo_now] + to_partners(mpo_now)).reshape(hi, states * states)
    shards = left_call(hi, lo, own_rows, here[None], dims_now, left_env[0])

    bits = [1 << b for b in range(1, n_sec.bit_length() - 1)]
    cut = sectors // 2

    def spread(first, second, waits):
        for t, (bit, other) in enumerate(zip(bits, bits[::-1])):
            if t > 0:
                first, second = lax.optimization_barrier((first, second, waits[t - 1]))[:2]
            first = jnp.concatenate([first, over_bit(first, bit)])
            second = jnp.concatenate([second, over_bit(second, other)])
        near = jnp.concatenate([first, second])
        return [near, over_bit(after(near, waits[-1]), 1)]

    gap = dest_owner[:, 0] ^ me
    up = sum(((gap // bit) % 2) << t for t, bit in enumerate(bits))
    down = sum(((gap // bit) % 2) << t for t, bit in enumerate(bits[::-1]))
    is_near = 1 - gap % 2
    row = jnp.where(
        left_slot < cut,
        up * cut + left_slot,
        (n_sec // 2) * cut + down * (sectors - cut) + left_slot - cut,
    )

    swapped = [[over_hi(shards[i][:cut], i), over_hi(shards[i][cut:], i)] for i in range(1, hi)]
    lefts = [lax.all_gather(shards[0], "sec", axis=0, tiled=True)]
    moved = [to_partners(after(pieces[0], swapped))]
    moved.append(to_partners(after(pieces[1], moved[0])))
    moved.append(to_partners(after(pieces[2], moved[1])))
    for first, second in swapped:
        first, second = lax.optimization_barrier((first, second, mpo_all))[:2]
        lefts += spread(first, second, moved[:2])
    most_wide = lax.pmax(after(n_wide, moved[1]), "sec")[0]
    mpo_all = after(mpo_all, most_wide)
    scalars = (order, right_dims, is_near, row, dest_owner[:, 0] * sectors + left_slot)

    def compute(span, narrow, scalars, lefts, mpo_all, others):
        return blocks_call(
            hi, lo, own_rows, narrow, span, scalars, mpo_all, psi, lefts, right, others
        )

    def exchange(send):
        return [over_lo(send[j - 1], j) for j in range(1, lo)]

    terms = []
    for m in range(2):
        keep, send = compute(early[m], False, scalars, lefts, mpo_all, moved[m])
        terms.append([keep] + exchange(send))

    def run(cap, scalars, moved, pieces, lefts, mpo_all, terms):
        order = scalars[0]
        moved, terms = list(moved), list(terms)
        spans = [(span, False) for span in early]
        sends = [pieces[0]]
        for a in range(fixed, cap, step):
            spans.append((slice(a, min(a + step, cap)), False))
        rest = blocks - cap
        count = -(-rest // (step + 1))
        for q in range(count):
            spans.append((slice(cap + rest * q // count, cap + rest * (q + 1) // count), True))
        for span, narrow in spans[len(early) :]:
            across = half if narrow else width
            sends.append(pieces[1][span.start - fixed : span.stop - fixed, :across, :across])
        total, done = len(spans), len(moved)
        for m in range(done, min(done + 2, total)):
            moved.append(to_partners(sends[m - done]))
        shape = (blocks, states, own_rows, width)
        out, added = None, 0
        for m in range(len(terms), total):
            if added < m - 1:
                out = add_call(shape, spans[added][0], order, terms[added], out)
                added += 1
                mpo_now, out = lax.optimization_barrier((mpo_all, out))
            keep, send = compute(*spans[m], scalars, lefts, mpo_now, moved[m])
            terms.append([keep] + exchange(send))
            if len(moved) < total:
                waits = (moved[-2], keep)
                moved.append(to_partners(after(sends[len(moved) - done], waits)))
        for m in range(added, total):
            out = add_call(shape, spans[m][0], order, terms[m], out)
        return out

    caps = sorted({max(fixed, blocks * q // 12) for q in (7, 8, 9)} | {blocks})
    which = sum((most_wide > cap).astype(jnp.int32) for cap in caps[:-1])
    return lax.switch(
        which,
        [functools.partial(run, cap) for cap in caps],
        scalars, moved, pieces[3:], lefts, mpo_all, terms,
    )


def solution(mesh):
    in_specs = (
        P("sec", None, None, None),
        P("chan", None, None),
        P("chan", "sec", None, None),
        P("chan", "sec", None, None),
        P("sec"),
        P("sec"),
        P("sec", None),
        P("sec"),
    )
    out_specs = P("sec", None, "chan", None)
    return jax.shard_map(
        functools.partial(on_device, mesh.shape["chan"], mesh.shape["sec"]),
        mesh=mesh,
        in_specs=in_specs,
        out_specs=out_specs,
        check_vma=False,
    )
```

```python
import functools

import jax
import jax.numpy as jnp
from jax import lax
from jax.experimental import pallas as pl
from jax.experimental.pallas import tpu as pltpu
from jax.sharding import PartitionSpec as P

ANY = pl.BlockSpec(memory_space=pl.ANY)
SMEM = pl.BlockSpec(memory_space=pltpu.SMEM)


def after(x, *others):
    return lax.optimization_barrier((x, others))[0]


def left_kernel(hi, lo, here, dims, left, *outs):
    own = outs[0].shape[1] // lo
    h, l = here[0] // lo, here[0] % lo
    r = dims[pl.program_id(0)]
    for i in range(hi):
        for j in range(lo):
            start = pl.multiple_of((((h + i) % hi) * lo + (l + j) % lo) * own, own)
            piece = left[0, pl.ds(start, own), :]
            inside = (lax.broadcasted_iota(jnp.int32, piece.shape, 0) + start < r) & (
                lax.broadcasted_iota(jnp.int32, piece.shape, 1) < r
            )
            outs[i][0, j * own : (j + 1) * own] = jnp.where(inside, piece, jnp.zeros_like(piece))


def left_call(hi, lo, own_rows, here, dims, left):
    sectors, width = left.shape[:2]
    block = (1, lo * own_rows, width)
    return pl.pallas_call(
        functools.partial(left_kernel, hi, lo),
        grid_spec=pltpu.PrefetchScalarGridSpec(
            num_scalar_prefetch=2,
            grid=(sectors,),
            in_specs=[pl.BlockSpec((1, width, width), lambda s, *_: (s, 0, 0))],
            out_specs=[pl.BlockSpec(block, lambda s, *_: (s, 0, 0))] * hi,
        ),
        out_shape=[jax.ShapeDtypeStruct((sectors,) + block[1:], left.dtype)] * hi,
        compiler_params=pltpu.CompilerParams(vmem_limit_bytes=32 * 2**20),
        cost_estimate=pl.CostEstimate(flops=left.size, bytes_accessed=4 * left.size, transcendentals=0),
    )(here, dims, left)


def plan_kernel(half, dims, order, count):
    blocks = dims.shape[0]

    def place(keep_wide):
        def body(k, at):
            mine = (dims[k] > half) == keep_wide

            @pl.when(mine)
            def _():
                order[at] = k

            return at + mine.astype(jnp.int32)

        return body

    wide = lax.fori_loop(0, blocks, place(True), jnp.int32(0))
    count[0] = wide
    lax.fori_loop(0, blocks, place(False), wide)


def plan_call(half, dims):
    return pl.pallas_call(
        functools.partial(plan_kernel, half),
        in_specs=[SMEM],
        out_specs=[SMEM, SMEM],
        out_shape=[jax.ShapeDtypeStruct(dims.shape, jnp.int32), jax.ShapeDtypeStruct((1,), jnp.int32)],
        cost_estimate=pl.CostEstimate(flops=0, bytes_accessed=4 * dims.size, transcendentals=0),
    )(dims)


def block_kernel(hi, rows, narrow, first, order, right_dims, sector, mpo, psi, left, *refs):
    rights = refs[:hi]
    keep, send = refs[hi:]
    states = psi.shape[1]
    k = order[pl.program_id(0) + first]
    stacked = left[0]
    parts = [
        jnp.dot(stacked, psi[0, p], preferred_element_type=jnp.float32) for p in range(states)
    ]
    total = None
    for i in range(hi):
        right = rights[i][0]
        if not narrow:
            r = right_dims[k]
            inside = (lax.broadcasted_iota(jnp.int32, right.shape, 0) < r) & (
                lax.broadcasted_iota(jnp.int32, right.shape, 1) < r
            )
            right = jnp.where(inside, right, jnp.zeros_like(right))
        mixed = []
        for s in range(states):
            acc = None
            for p in range(states):
                piece = parts[p][i * rows : (i + 1) * rows] * mpo[i, s * states + p]
                acc = piece if acc is None else acc + piece
            mixed.append(acc.astype(jnp.bfloat16))
        mixed = jnp.concatenate(mixed, axis=0)
        product = lax.dot_general(
            mixed, right, (((1,), (1,)), ((), ())), preferred_element_type=jnp.float32
        )
        total = product if total is None else total + product
    own = keep.shape[2]
    for s in range(states):
        keep[0, s] = total[s * rows : s * rows + own].astype(keep.dtype)
        for j in range(send.shape[0]):
            at = s * rows + (j + 1) * own
            send[j, 0, s] = total[at : at + own].astype(send.dtype)


def blocks_call(hi, lo, own_rows, narrow, span, scalars, mpo, psi, left, right, others):
    states, width = psi.shape[1], psi.shape[2]
    first, count = span.start, span.stop - span.start
    across = width // 2 if narrow else width
    rows = lo * own_rows

    def by_block(k, order, *_):
        return (order[k + first], 0, 0)

    def by_sector(k, order, right_dims, sector, *_):
        return (sector[order[k + first]], 0, 0)

    grid_spec = pltpu.PrefetchScalarGridSpec(
        num_scalar_prefetch=4,
        grid=(count,),
        in_specs=[
            pl.BlockSpec((1, states, width, across), lambda *at: by_block(*at) + (0,)),
        ]
        + [pl.BlockSpec((1, hi * rows, width), by_sector)]
        + [pl.BlockSpec((1, across, across), by_block)]
        + [pl.BlockSpec((1, across, across), lambda k, *_: (k, 0, 0))] * (hi - 1),
        out_specs=[
            pl.BlockSpec((1, states, own_rows, across), lambda k, *_: (k, 0, 0, 0)),
            pl.BlockSpec((lo - 1, 1, states, own_rows, across), lambda k, *_: (0, k, 0, 0, 0)),
        ],
    )
    return pl.pallas_call(
        functools.partial(block_kernel, hi, rows, narrow, first),
        grid_spec=grid_spec,
        out_shape=[
            jax.ShapeDtypeStruct((count, states, own_rows, across), jnp.bfloat16),
            jax.ShapeDtypeStruct((lo - 1, count, states, own_rows, across), jnp.bfloat16),
        ],
        compiler_params=pltpu.CompilerParams(vmem_limit_bytes=40 * 2**20),
        cost_estimate=pl.CostEstimate(
            flops=count * 2 * hi * rows * states * across * (width + across),
            bytes_accessed=count * 5 * states * width * across,
            transcendentals=0,
        ),
    )(*scalars, mpo, psi, left, right, *others)


def add_kernel(terms, span, order, other, *refs):
    out, total, sems = refs[-3:]
    across = refs[0].shape[-1]
    copies = []
    for k in range(span.stop - span.start):
        acc = refs[0][k].astype(jnp.float32)
        for j in range(1, terms):
            acc = acc + refs[j][other[0] if refs[j].shape[0] > 1 else 0, k].astype(jnp.float32)
        total[k, :, :, :across] = acc.astype(total.dtype)
        if across < total.shape[-1]:
            total[k, :, :, across:] = jnp.zeros(acc.shape[:-1] + (total.shape[-1] - across,), total.dtype)
        copy = pltpu.make_async_copy(total.at[k], out.at[order[k + span.start]], sems.at[k])
        copy.start()
        copies.append(copy)
    for copy in copies:
        copy.wait()


def add_call(shape, span, order, other, terms, out):
    count = span.stop - span.start
    return pl.pallas_call(
        functools.partial(add_kernel, len(terms), span),
        in_specs=[SMEM, SMEM]
        + [pl.BlockSpec(memory_space=pltpu.VMEM)] * len(terms)
        + ([] if out is None else [ANY]),
        out_specs=ANY,
        out_shape=jax.ShapeDtypeStruct(shape, jnp.bfloat16),
        scratch_shapes=[
            pltpu.VMEM((count,) + shape[1:], jnp.bfloat16),
            pltpu.SemaphoreType.DMA((count,)),
        ],
        input_output_aliases={} if out is None else {2 + len(terms): 0},
        compiler_params=pltpu.CompilerParams(vmem_limit_bytes=24 * 2**20),
        cost_estimate=pl.CostEstimate(
            flops=terms[0].size, bytes_accessed=6 * terms[0].size, transcendentals=0
        ),
    )(order, other, *terms, *([] if out is None else [out]))


def on_device(n_chan, psi, mpo, left_env, right_env, left_dims, right_dims, dest_owner, left_slot):
    blocks, states, width = psi.shape[:3]
    sectors = left_env.shape[1]
    half = width // 2
    hi = 2 if n_chan % 2 == 0 else 1
    lo = n_chan // hi
    own_rows = width // n_chan
    here = lax.axis_index("chan")
    other = (lo - 1 - here % lo)[None]
    right = right_env[0]
    step = max(blocks // 6, 1)

    def over_hi(x, i):
        pairs = [(c, ((c // lo + i) % hi) * lo + c % lo) for c in range(n_chan)]
        return lax.ppermute(x, "chan", pairs)

    def over_lo(x, j):
        pairs = [(c, (c // lo) * lo + (c % lo + j) % lo) for c in range(n_chan)]
        return lax.ppermute(x, "chan", pairs)

    def to_partners(x):
        return [over_hi(x, i) for i in range(1, hi)]

    def exchange(send, aside):
        if aside and lo == 2:
            groups = [[h * lo, h * lo + 1] for h in range(hi)]
            return [lax.all_gather(send[0], "chan", axis_index_groups=groups, axis=0)]
        return [over_lo(send[j - 1], j)[None] for j in range(1, lo)]

    order, n_wide = plan_call(half, right_dims)
    scalars = (order, right_dims, dest_owner[:, 0] * sectors + left_slot)
    early = [slice(0, 2 * step), slice(2 * step, 3 * step)]
    fixed = early[-1].stop

    def piece(span, order, across=width):
        return jnp.take(right[:, :across, :across], order[span], axis=0, mode="clip")

    shards = left_call(hi, lo, own_rows, here[None], left_dims, left_env[0])
    swapped = [over_hi(shards[i], i) for i in range(1, hi)]
    mpo_all = jnp.stack([mpo[0]] + to_partners(mpo[0])).reshape(hi, states * states)
    left = lax.all_gather(jnp.concatenate([shards[0]] + swapped, axis=1), "sec", axis=0, tiled=True)
    moved = [to_partners(after(piece(span, order), swapped)) for span in early]
    most_wide = lax.pmax(after(n_wide, moved[0]), "sec")[0]
    mpo_all = after(mpo_all, most_wide)

    def compute(span, narrow, scalars, left, mpo_all, others):
        return blocks_call(
            hi, lo, own_rows, narrow, span, scalars, mpo_all, psi, left, right, others
        )

    first = compute(early[0], False, scalars, left, mpo_all, moved[0])

    def run(cap, scalars, moved, left, mpo_all, first):
        order = scalars[0]
        moved = list(moved)
        spans = [(span, False) for span in early]
        for a in range(fixed, cap, step):
            spans.append((slice(a, min(a + step, cap)), False))
        rest = blocks - cap
        count = -(-rest // (step + 1))
        for q in range(count):
            spans.append((slice(cap + rest * q // count, cap + rest * (q + 1) // count), True))
        total = len(spans)

        def next_piece():
            span, narrow = spans[len(moved)]
            return piece(span, order, half if narrow else width)

        while len(moved) < min(4, total):
            moved.append(to_partners(next_piece()))
        shape = (blocks, states, own_rows, width)
        out, added = None, 0
        terms = [[first[0]] + exchange(first[1], True)]
        mpo_now = mpo_all
        for m in range(1, total):
            if m > 2:
                out = add_call(shape, spans[added][0], order, other, terms[added], out)
                added += 1
                mpo_now, out = lax.optimization_barrier((mpo_all, out))
            keep, send = compute(*spans[m], scalars, left, mpo_now, moved[m])
            terms.append([keep] + exchange(send, m < 2))
            if len(moved) < total:
                waits = (moved[-2], keep)
                moved.append(to_partners(after(next_piece(), waits)))
        for m in range(added, total):
            out = add_call(shape, spans[m][0], order, other, terms[m], out)
        return out

    caps = sorted({max(fixed, blocks * q // 12) for q in (7, 8, 9)} | {blocks})
    which = sum((most_wide > cap).astype(jnp.int32) for cap in caps[:-1])
    return lax.switch(
        which, [functools.partial(run, cap) for cap in caps], scalars, moved, left, mpo_all, first
    )


def solution(mesh):
    in_specs = (
        P("sec", None, None, None),
        P("chan", None, None),
        P("chan", "sec", None, None),
        P("chan", "sec", None, None),
        P("sec"),
        P("sec"),
        P("sec", None),
        P("sec"),
    )
    out_specs = P("sec", None, "chan", None)
    return jax.shard_map(
        functools.partial(on_device, mesh.shape["chan"]),
        mesh=mesh,
        in_specs=in_specs,
        out_specs=out_specs,
        check_vma=False,
    )
```

```python
import functools

import jax
import jax.numpy as jnp
from jax import lax
from jax.experimental import pallas as pl
from jax.experimental.pallas import tpu as pltpu
from jax.sharding import PartitionSpec as P

ANY = pl.BlockSpec(memory_space=pl.ANY)
SMEM = pl.BlockSpec(memory_space=pltpu.SMEM)


def after(x, *others):
    return lax.optimization_barrier((x, others))[0]


def digits(c, parity, hi, lo):
    return (c // lo, c % lo) if parity == 0 else (c % hi, c // hi)


def rank(h, l, parity, hi, lo):
    return h * lo + l if parity == 0 else l * hi + h


def left_kernel(hi, lo, where, own_dims, side_dims, own_left, side_left, *outs):
    own = outs[0].shape[1] // lo
    sectors = own_dims.shape[0]
    s = pl.program_id(0)
    here, odd = where[0], where[1] == 1
    h = jnp.where(odd, here % hi, here // lo)
    l = jnp.where(odd, here // hi, here % lo)
    r = jnp.where(s < sectors, own_dims[s % sectors], side_dims[s % sectors])
    first = jnp.full((own, own_left.shape[2]), (s < sectors).astype(jnp.int32)) > 0
    for i in range(hi):
        for j in range(lo):
            hh, ll = (h + i) % hi, (l + j) % lo
            start = pl.multiple_of(jnp.where(odd, ll * hi + hh, hh * lo + ll) * own, own)
            piece = jnp.where(first, own_left[0, pl.ds(start, own), :], side_left[0, pl.ds(start, own), :])
            inside = (lax.broadcasted_iota(jnp.int32, piece.shape, 0) + start < r) & (
                lax.broadcasted_iota(jnp.int32, piece.shape, 1) < r
            )
            outs[i][0, j * own : (j + 1) * own] = jnp.where(inside, piece, jnp.zeros_like(piece))


def left_call(hi, lo, own_rows, where, own_dims, side_dims, own_left, side_left):
    sectors, width = own_left.shape[:2]
    block = (1, lo * own_rows, width)
    return pl.pallas_call(
        functools.partial(left_kernel, hi, lo),
        grid_spec=pltpu.PrefetchScalarGridSpec(
            num_scalar_prefetch=3,
            grid=(2 * sectors,),
            in_specs=[
                pl.BlockSpec((1, width, width), lambda s, *_: (jnp.minimum(s, sectors - 1), 0, 0)),
                pl.BlockSpec((1, width, width), lambda s, *_: (jnp.maximum(s - sectors, 0), 0, 0)),
            ],
            out_specs=[pl.BlockSpec(block, lambda s, *_: (s, 0, 0))] * hi,
        ),
        out_shape=[jax.ShapeDtypeStruct((2 * sectors,) + block[1:], own_left.dtype)] * hi,
        compiler_params=pltpu.CompilerParams(vmem_limit_bytes=32 * 2**20),
        cost_estimate=pl.CostEstimate(
            flops=2 * own_left.size, bytes_accessed=8 * own_left.size, transcendentals=0
        ),
    )(where, own_dims, side_dims, own_left, side_left)


def plan_kernel(half, dims, order, count):
    blocks = dims.shape[0]

    def place(keep_wide):
        def body(k, at):
            mine = (dims[k] > half) == keep_wide

            @pl.when(mine)
            def _():
                order[at] = k

            return at + mine.astype(jnp.int32)

        return body

    wide = lax.fori_loop(0, blocks, place(True), jnp.int32(0))
    count[0] = wide
    lax.fori_loop(0, blocks, place(False), wide)


def plan_call(half, dims):
    return pl.pallas_call(
        functools.partial(plan_kernel, half),
        in_specs=[SMEM],
        out_specs=[SMEM, SMEM],
        out_shape=[jax.ShapeDtypeStruct(dims.shape, jnp.int32), jax.ShapeDtypeStruct((1,), jnp.int32)],
        cost_estimate=pl.CostEstimate(flops=0, bytes_accessed=4 * dims.size, transcendentals=0),
    )(dims)


def block_kernel(hi, rows, narrow, first, order, right_dims, sector, mpo, psi, *refs):
    lefts, rights = refs[:hi], refs[hi : 2 * hi]
    keep, send = refs[2 * hi :]
    states = psi.shape[1]
    k = order[pl.program_id(0) + first]
    stacked = jnp.concatenate([left[0] for left in lefts], axis=0)
    parts = [
        jnp.dot(stacked, psi[0, p], preferred_element_type=jnp.float32) for p in range(states)
    ]
    total = None
    for i in range(hi):
        right = rights[i][0]
        if not narrow:
            r = right_dims[k]
            inside = (lax.broadcasted_iota(jnp.int32, right.shape, 0) < r) & (
                lax.broadcasted_iota(jnp.int32, right.shape, 1) < r
            )
            right = jnp.where(inside, right, jnp.zeros_like(right))
        mixed = []
        for s in range(states):
            acc = None
            for p in range(states):
                piece = parts[p][i * rows : (i + 1) * rows] * mpo[i, s * states + p]
                acc = piece if acc is None else acc + piece
            mixed.append(acc.astype(jnp.bfloat16))
        mixed = jnp.concatenate(mixed, axis=0)
        product = lax.dot_general(
            mixed, right, (((1,), (1,)), ((), ())), preferred_element_type=jnp.float32
        )
        total = product if total is None else total + product
    own = keep.shape[2]
    for s in range(states):
        keep[0, s] = total[s * rows : s * rows + own].astype(keep.dtype)
        for j in range(send.shape[0]):
            at = s * rows + (j + 1) * own
            send[j, 0, s] = total[at : at + own].astype(send.dtype)


def blocks_call(hi, lo, own_rows, narrow, span, base, scalars, mpo, psi, lefts, right, others):
    states, width = psi.shape[1], psi.shape[2]
    first, count = span.start, span.stop - span.start
    across = width // 2 if narrow else width
    rows = lo * own_rows

    def by_block(k, order, *_):
        return (order[k + first], 0, 0)

    def by_sector(k, order, right_dims, sector, *_):
        return (sector[order[k + first]], 0, 0)

    grid_spec = pltpu.PrefetchScalarGridSpec(
        num_scalar_prefetch=4,
        grid=(count,),
        in_specs=[
            pl.BlockSpec((1, states, width, across), lambda *at: by_block(*at) + (0,)),
        ]
        + [pl.BlockSpec((1, rows, width), by_sector)] * hi
        + [pl.BlockSpec((1, across, across), by_block)]
        + [pl.BlockSpec((1, across, across), lambda k, *_: (k + first - base, 0, 0))] * (hi - 1),
        out_specs=[
            pl.BlockSpec((1, states, own_rows, across), lambda k, *_: (k, 0, 0, 0)),
            pl.BlockSpec((lo - 1, 1, states, own_rows, across), lambda k, *_: (0, k, 0, 0, 0)),
        ],
    )
    return pl.pallas_call(
        functools.partial(block_kernel, hi, rows, narrow, first),
        grid_spec=grid_spec,
        out_shape=[
            jax.ShapeDtypeStruct((count, states, own_rows, across), jnp.bfloat16),
            jax.ShapeDtypeStruct((lo - 1, count, states, own_rows, across), jnp.bfloat16),
        ],
        compiler_params=pltpu.CompilerParams(vmem_limit_bytes=40 * 2**20),
        cost_estimate=pl.CostEstimate(
            flops=count * 2 * hi * rows * states * across * (width + across),
            bytes_accessed=count * 5 * states * width * across,
            transcendentals=0,
        ),
    )(*scalars, mpo, psi, *lefts, right, *others)


def add_kernel(terms, span, order, *refs):
    out, total, sems = refs[-3:]
    across = refs[0].shape[-1]
    copies = []
    for k in range(span.stop - span.start):
        acc = refs[0][k].astype(jnp.float32)
        for j in range(1, terms):
            acc = acc + refs[j][k].astype(jnp.float32)
        total[k, :, :, :across] = acc.astype(total.dtype)
        if across < total.shape[-1]:
            total[k, :, :, across:] = jnp.zeros(acc.shape[:-1] + (total.shape[-1] - across,), total.dtype)
        copy = pltpu.make_async_copy(total.at[k], out.at[order[k + span.start]], sems.at[k])
        copy.start()
        copies.append(copy)
    for copy in copies:
        copy.wait()


def add_call(shape, span, order, terms, out):
    count = span.stop - span.start
    return pl.pallas_call(
        functools.partial(add_kernel, len(terms), span),
        in_specs=[SMEM]
        + [pl.BlockSpec(memory_space=pltpu.VMEM)] * len(terms)
        + ([] if out is None else [ANY]),
        out_specs=ANY,
        out_shape=jax.ShapeDtypeStruct(shape, jnp.bfloat16),
        scratch_shapes=[
            pltpu.VMEM((count,) + shape[1:], jnp.bfloat16),
            pltpu.SemaphoreType.DMA((count,)),
        ],
        input_output_aliases={} if out is None else {1 + len(terms): 0},
        compiler_params=pltpu.CompilerParams(vmem_limit_bytes=24 * 2**20),
        cost_estimate=pl.CostEstimate(
            flops=terms[0].size, bytes_accessed=6 * terms[0].size, transcendentals=0
        ),
    )(order, *terms, *([] if out is None else [out]))


def on_device(n_chan, n_sec, psi, mpo, left_env, right_env, left_dims, right_dims, dest_owner, left_slot):
    blocks, states, width = psi.shape[:3]
    sectors = left_env.shape[1]
    half = width // 2
    hi = 2 if n_chan % 2 == 0 else 1
    lo = n_chan // hi
    own_rows = width // n_chan
    here, me = lax.axis_index("chan"), lax.axis_index("sec")
    odd = me % 2
    right = right_env[0]
    step = max(blocks // 6, 1)

    def route(x, up, along):
        pairs = []
        for c in range(n_chan):
            for s in range(n_sec):
                h, l = digits(c, s % 2, hi, lo)
                to = rank((h + up) % hi, (l + along) % lo, s % 2, hi, lo)
                pairs.append((c * n_sec + s, to * n_sec + s))
        return lax.ppermute(x, ("chan", "sec"), pairs)

    def to_partners(x):
        return [route(x, i, 0) for i in range(1, hi)]

    def beside(x):
        return lax.ppermute(x, "sec", [(s, s ^ 1) for s in range(n_sec)])

    side_left, side_dims = beside(left_env[0]), beside(left_dims)
    mpo_all = jnp.stack([mpo[0]] + to_partners(mpo[0])).reshape(hi, states * states)
    order, n_wide = plan_call(half, right_dims)
    most_wide = lax.pmax(n_wide, "sec")[0]
    shards = left_call(
        hi, lo, own_rows, jnp.stack([here, odd]).astype(jnp.int32),
        left_dims, side_dims, left_env[0], side_left,
    )
    owner = dest_owner[:, 0]
    sector = (owner // 2) * (2 * sectors) + ((owner % 2) ^ odd) * sectors + left_slot
    scalars = (order, right_dims, sector)

    def gathered(x):
        groups = [list(range(parity, n_sec, 2)) for parity in range(2)]
        return lax.all_gather(x, "sec", axis_index_groups=groups, axis=0, tiled=True)

    def run(cap, scalars, shards, mpo_all):
        order = scalars[0]
        swapped = [route(shards[i], i, 0) for i in range(1, hi)]
        lefts = [gathered(shards[0])] + [gathered(x) for x in swapped]
        spans = [(slice(a, min(a + step, cap)), False) for a in range(0, cap, step)]
        rest = blocks - cap
        count = -(-rest // (step + 1))
        for q in range(count):
            spans.append((slice(cap + rest * q // count, cap + rest * (q + 1) // count), True))
        total = len(spans)
        wide = jnp.take(right, order[:cap], axis=0, mode="clip")
        moved = [to_partners(after(wide, swapped))]
        if rest:
            thin = jnp.take(right[:, :half, :half], order[cap:], axis=0, mode="clip")
            moved.append(to_partners(after(thin, swapped)))
        shape = (blocks, states, own_rows, width)
        out, added, terms = None, 0, []
        mpo_now = mpo_all
        for m in range(total):
            if m > 3:
                out = add_call(shape, spans[added][0], order, terms[added], out)
                added += 1
                mpo_now, out = lax.optimization_barrier((mpo_all, out))
            span, narrow = spans[m]
            keep, send = blocks_call(
                hi, lo, own_rows, narrow, span, cap if narrow else 0, scalars, mpo_now, psi,
                lefts, right, moved[1 if narrow else 0],
            )
            terms.append([keep] + [route(send[j - 1], 0, j) for j in range(1, lo)])
        for m in range(added, total):
            out = add_call(shape, spans[m][0], order, terms[m], out)
        return out

    caps = sorted({max(1, blocks * q // 12) for q in (7, 8, 9)} | {blocks})
    which = sum((most_wide > cap).astype(jnp.int32) for cap in caps[:-1])
    return lax.switch(
        which, [functools.partial(run, cap) for cap in caps], scalars, shards, mpo_all
    )


def solution(mesh):
    in_specs = (
        P("sec", None, None, None),
        P("chan", None, None),
        P("chan", "sec", None, None),
        P("chan", "sec", None, None),
        P("sec"),
        P("sec"),
        P("sec", None),
        P("sec"),
    )
    out_specs = P("sec", None, "chan", None)
    return jax.shard_map(
        functools.partial(on_device, mesh.shape["chan"], mesh.shape["sec"]),
        mesh=mesh,
        in_specs=in_specs,
        out_specs=out_specs,
        check_vma=False,
    )
```

```python
import functools

import jax
import jax.numpy as jnp
from jax import lax
from jax.experimental import pallas as pl
from jax.experimental.pallas import tpu as pltpu
from jax.sharding import PartitionSpec as P

ANY = pl.BlockSpec(memory_space=pl.ANY)
SMEM = pl.BlockSpec(memory_space=pltpu.SMEM)


def after(x, *others):
    return lax.optimization_barrier((x, others))[0]


def digits(c, parity, hi, lo):
    return (c // lo, c % lo) if parity == 0 else (c % hi, c // hi)


def rank(h, l, parity, hi, lo):
    return h * lo + l if parity == 0 else l * hi + h


def left_kernel(hi, lo, where, own_dims, side_dims, own_left, side_left, *outs):
    own = outs[0].shape[1] // lo
    sectors, each = own_dims.shape[0], own_left.shape[0]
    step = pl.program_id(0)
    here, odd = where[0], where[1] == 1
    h = jnp.where(odd, here % hi, here // lo)
    l = jnp.where(odd, here // hi, here % lo)

    def fill(left, dims, at):
        for n in range(each):
            r = dims[at * each + n]
            for i in range(hi):
                for j in range(lo):
                    hh, ll = (h + i) % hi, (l + j) % lo
                    start = pl.multiple_of(jnp.where(odd, ll * hi + hh, hh * lo + ll) * own, own)
                    piece = left[n, pl.ds(start, own), :]
                    inside = (lax.broadcasted_iota(jnp.int32, piece.shape, 0) + start < r) & (
                        lax.broadcasted_iota(jnp.int32, piece.shape, 1) < r
                    )
                    outs[i][n, j * own : (j + 1) * own] = jnp.where(
                        inside, piece, jnp.zeros_like(piece)
                    )

    half = sectors // each

    @pl.when(step < half)
    def _():
        fill(own_left, own_dims, step)

    @pl.when(step >= half)
    def _():
        fill(side_left, side_dims, step - half)


def left_call(hi, lo, own_rows, where, own_dims, side_dims, own_left, side_left):
    sectors, width = own_left.shape[:2]
    each = 4 if sectors % 4 == 0 else 1
    half = sectors // each
    block = (each, lo * own_rows, width)
    return pl.pallas_call(
        functools.partial(left_kernel, hi, lo),
        grid_spec=pltpu.PrefetchScalarGridSpec(
            num_scalar_prefetch=3,
            grid=(2 * half,),
            in_specs=[
                pl.BlockSpec((each, width, width), lambda s, *_: (jnp.minimum(s, half - 1), 0, 0)),
                pl.BlockSpec((each, width, width), lambda s, *_: (jnp.maximum(s - half, 0), 0, 0)),
            ],
            out_specs=[pl.BlockSpec(block, lambda s, *_: (s, 0, 0))] * hi,
        ),
        out_shape=[jax.ShapeDtypeStruct((2 * sectors,) + block[1:], own_left.dtype)] * hi,
        compiler_params=pltpu.CompilerParams(vmem_limit_bytes=32 * 2**20),
        cost_estimate=pl.CostEstimate(
            flops=2 * own_left.size, bytes_accessed=8 * own_left.size, transcendentals=0
        ),
    )(where, own_dims, side_dims, own_left, side_left)


def plan_kernel(half, sectors, slots, me, dims, table, order, near, row, asked, seen):
    blocks = dims.shape[0]
    n_sec = table.shape[0]
    chips = n_sec // 2
    mine, parity = me[0] // 2, me[0] % 2

    def local(want):
        owner = want // sectors
        return ((owner % 2) ^ parity) * sectors + want % sectors

    def place(keep_wide):
        def body(k, at):
            fits = (dims[k] > half) == keep_wide

            @pl.when(fits)
            def _():
                order[at] = k

            return at + fits.astype(jnp.int32)

        return body

    wide = lax.fori_loop(0, blocks, place(True), jnp.int32(0))
    lax.fori_loop(0, blocks, place(False), wide)

    for chip in range(chips):
        seen[chip] = 0

    def source(k, _):
        want = table[me[0], k]
        chip = want // sectors // 2
        here = chip == mine
        count = seen[chip]
        seen[chip] = count + 1
        near[k] = here.astype(jnp.int32)
        far = ((chip ^ mine) - 1) * slots + jnp.minimum(count, slots - 1)
        row[k] = jnp.where(here, local(want), far)
        return 0

    lax.fori_loop(0, blocks, source, 0)

    for gap in range(1, chips):
        base = (gap - 1) * slots
        for n in range(slots):
            asked[base + n] = 0
        dest = (mine ^ gap) * 2 + parity

        def wish(k, count):
            want = table[dest, k]
            here = want // sectors // 2 == mine

            @pl.when(here)
            def _():
                asked[base + jnp.minimum(count, slots - 1)] = local(want)

            return count + here.astype(jnp.int32)

        lax.fori_loop(0, blocks, wish, jnp.int32(0))


def plan_call(half, sectors, slots, me, dims, table):
    blocks, chips = dims.shape[0], table.shape[0] // 2
    ints = [blocks, blocks, blocks, max(chips - 1, 1) * slots]
    return pl.pallas_call(
        functools.partial(plan_kernel, half, sectors, slots),
        in_specs=[SMEM] * 3,
        out_specs=[SMEM] * 4,
        out_shape=[jax.ShapeDtypeStruct((n,), jnp.int32) for n in ints],
        scratch_shapes=[pltpu.SMEM((chips,), jnp.int32)],
        cost_estimate=pl.CostEstimate(flops=0, bytes_accessed=4 * table.size, transcendentals=0),
    )(me, dims, table)


def block_kernel(hi, rows, narrow, first, order, right_dims, near, row, mpo, psi, *refs):
    lefts, rights = refs[: 2 * hi], refs[2 * hi : 3 * hi]
    keep, send = refs[3 * hi :]
    states = psi.shape[1]
    k = order[pl.program_id(0) + first]
    is_near = jnp.full(lefts[0].shape[1:], near[k], jnp.int32) > 0
    stacked = jnp.concatenate(
        [jnp.where(is_near, lefts[2 * i][0], lefts[2 * i + 1][0]) for i in range(hi)], axis=0
    )
    parts = [
        jnp.dot(stacked, psi[0, p], preferred_element_type=jnp.float32) for p in range(states)
    ]
    total = None
    for i in range(hi):
        right = rights[i][0]
        if not narrow:
            r = right_dims[k]
            inside = (lax.broadcasted_iota(jnp.int32, right.shape, 0) < r) & (
                lax.broadcasted_iota(jnp.int32, right.shape, 1) < r
            )
            right = jnp.where(inside, right, jnp.zeros_like(right))
        mixed = []
        for s in range(states):
            acc = None
            for p in range(states):
                piece = parts[p][i * rows : (i + 1) * rows] * mpo[i, s * states + p]
                acc = piece if acc is None else acc + piece
            mixed.append(acc.astype(jnp.bfloat16))
        mixed = jnp.concatenate(mixed, axis=0)
        product = lax.dot_general(
            mixed, right, (((1,), (1,)), ((), ())), preferred_element_type=jnp.float32
        )
        total = product if total is None else total + product
    own = keep.shape[2]
    for s in range(states):
        keep[0, s] = total[s * rows : s * rows + own].astype(keep.dtype)
        for j in range(send.shape[0]):
            at = s * rows + (j + 1) * own
            send[j, 0, s] = total[at : at + own].astype(send.dtype)


def blocks_call(hi, lo, own_rows, narrow, span, base, scalars, mpo, psi, lefts, right, others):
    states, width = psi.shape[1], psi.shape[2]
    first, count = span.start, span.stop - span.start
    across = width // 2 if narrow else width
    rows = lo * own_rows

    def by_block(k, order, *_):
        return (order[k + first], 0, 0)

    def by_row(far):
        def index(k, order, right_dims, near, row, *_):
            block = order[k + first]
            return (jnp.where(near[block] == 1 - far, row[block], 0), 0, 0)

        return index

    grid_spec = pltpu.PrefetchScalarGridSpec(
        num_scalar_prefetch=5,
        grid=(count,),
        in_specs=[
            pl.BlockSpec((1, states, width, across), lambda *at: by_block(*at) + (0,)),
        ]
        + [pl.BlockSpec((1, rows, width), by_row(far)) for _ in range(hi) for far in range(2)]
        + [pl.BlockSpec((1, across, across), by_block)]
        + [pl.BlockSpec((1, across, across), lambda k, *_: (k + first - base, 0, 0))] * (hi - 1),
        out_specs=[
            pl.BlockSpec((1, states, own_rows, across), lambda k, *_: (k, 0, 0, 0)),
            pl.BlockSpec((lo - 1, 1, states, own_rows, across), lambda k, *_: (0, k, 0, 0, 0)),
        ],
    )
    return pl.pallas_call(
        functools.partial(block_kernel, hi, rows, narrow, first),
        grid_spec=grid_spec,
        out_shape=[
            jax.ShapeDtypeStruct((count, states, own_rows, across), jnp.bfloat16),
            jax.ShapeDtypeStruct((lo - 1, count, states, own_rows, across), jnp.bfloat16),
        ],
        compiler_params=pltpu.CompilerParams(vmem_limit_bytes=40 * 2**20),
        cost_estimate=pl.CostEstimate(
            flops=count * 2 * hi * rows * states * across * (width + across),
            bytes_accessed=count * 5 * states * width * across,
            transcendentals=0,
        ),
    )(*scalars, mpo, psi, *lefts, right, *others)


def add_kernel(terms, span, order, *refs):
    out, total, sems = refs[-3:]
    across = refs[0].shape[-1]
    copies = []
    for k in range(span.stop - span.start):
        acc = refs[0][k].astype(jnp.float32)
        for j in range(1, terms):
            acc = acc + refs[j][k].astype(jnp.float32)
        total[k, :, :, :across] = acc.astype(total.dtype)
        if across < total.shape[-1]:
            total[k, :, :, across:] = jnp.zeros(acc.shape[:-1] + (total.shape[-1] - across,), total.dtype)
        copy = pltpu.make_async_copy(total.at[k], out.at[order[k + span.start]], sems.at[k])
        copy.start()
        copies.append(copy)
    for copy in copies:
        copy.wait()


def add_call(shape, span, order, terms, out):
    count = span.stop - span.start
    return pl.pallas_call(
        functools.partial(add_kernel, len(terms), span),
        in_specs=[SMEM]
        + [pl.BlockSpec(memory_space=pltpu.VMEM)] * len(terms)
        + ([] if out is None else [ANY]),
        out_specs=ANY,
        out_shape=jax.ShapeDtypeStruct(shape, jnp.bfloat16),
        scratch_shapes=[
            pltpu.VMEM((count,) + shape[1:], jnp.bfloat16),
            pltpu.SemaphoreType.DMA((count,)),
        ],
        input_output_aliases={} if out is None else {1 + len(terms): 0},
        compiler_params=pltpu.CompilerParams(vmem_limit_bytes=24 * 2**20),
        cost_estimate=pl.CostEstimate(
            flops=terms[0].size, bytes_accessed=6 * terms[0].size, transcendentals=0
        ),
    )(order, *terms, *([] if out is None else [out]))


def on_device(n_chan, n_sec, psi, mpo, left_env, right_env, left_dims, right_dims, dest_owner, left_slot):
    blocks, states, width = psi.shape[:3]
    sectors = left_env.shape[1]
    half = width // 2
    hi = 2 if n_chan % 2 == 0 else 1
    lo = n_chan // hi
    own_rows = width // n_chan
    here, me = lax.axis_index("chan"), lax.axis_index("sec")
    odd = me % 2
    right = right_env[0]
    step = max(blocks // 6, 1)

    def route(x, up, along):
        pairs = []
        for c in range(n_chan):
            for s in range(n_sec):
                h, l = digits(c, s % 2, hi, lo)
                to = rank((h + up) % hi, (l + along) % lo, s % 2, hi, lo)
                pairs.append((c * n_sec + s, to * n_sec + s))
        return lax.ppermute(x, ("chan", "sec"), pairs)

    def to_partners(x):
        return [route(x, i, 0) for i in range(1, hi)]

    def beside(x):
        return lax.ppermute(x, "sec", [(s, s ^ 1) for s in range(n_sec)])

    side_left, side_dims = beside(left_env[0]), beside(left_dims)
    mpo_all = jnp.stack([mpo[0]] + to_partners(mpo[0])).reshape(hi, states * states)
    slots = 2 * -(-blocks // n_sec)
    wants = dest_owner[:, 0] * sectors + left_slot
    n_wide = jnp.sum((right_dims > half).astype(jnp.int32))[None]
    mine = jnp.arange(n_sec, dtype=jnp.int32)[:, None] == me
    table = lax.psum(jnp.where(mine, jnp.concatenate([wants, n_wide])[None], 0), "sec")
    most_wide = jnp.max(table[:, blocks])
    order, near, row, asked = plan_call(half, sectors, slots, me[None], right_dims, table)
    shards = left_call(
        hi, lo, own_rows, jnp.stack([here, odd]).astype(jnp.int32),
        left_dims, side_dims, left_env[0], side_left,
    )
    scalars = (order, right_dims, near, row)

    def fetched(x, asked):
        parts = []
        for gap in range(1, n_sec // 2):
            packed = jnp.take(x, asked[(gap - 1) * slots : gap * slots], axis=0, mode="clip")
            parts.append(lax.ppermute(packed, "sec", [(s, s ^ (2 * gap)) for s in range(n_sec)]))
        return jnp.concatenate(parts, axis=0)

    def run(cap, scalars, asked, shards, mpo_all):
        order = scalars[0]
        swapped = [route(shards[i], i, 0) for i in range(1, hi)]
        lefts = []
        for x in [shards[0]] + swapped:
            lefts += [x, fetched(x, asked)]
        spans = [(slice(a, min(a + step, cap)), False) for a in range(0, cap, step)]
        rest = blocks - cap
        count = -(-rest // (step + 1))
        for q in range(count):
            spans.append((slice(cap + rest * q // count, cap + rest * (q + 1) // count), True))
        total = len(spans)
        wide = jnp.take(right, order[:cap], axis=0, mode="clip")
        moved = [to_partners(after(wide, swapped))]
        if rest:
            thin = jnp.take(right[:, :half, :half], order[cap:], axis=0, mode="clip")
            moved.append(to_partners(after(thin, swapped)))
            mpo_all = after(mpo_all, moved[1])
        shape = (blocks, states, own_rows, width)
        out, added, terms = None, 0, []
        mpo_now = mpo_all
        for m in range(total):
            if m > 3:
                out = add_call(shape, spans[added][0], order, terms[added], out)
                added += 1
                mpo_now, out = lax.optimization_barrier((mpo_all, out))
            span, narrow = spans[m]
            keep, send = blocks_call(
                hi, lo, own_rows, narrow, span, cap if narrow else 0, scalars, mpo_now, psi,
                lefts, right, moved[1 if narrow else 0],
            )
            terms.append([keep] + [route(send[j - 1], 0, j) for j in range(1, lo)])
        for m in range(added, total):
            out = add_call(shape, spans[m][0], order, terms[m], out)
        return out

    caps = sorted({max(1, blocks * q // 12) for q in (7, 8, 9)} | {blocks})
    which = sum((most_wide > cap).astype(jnp.int32) for cap in caps[:-1])
    return lax.switch(
        which, [functools.partial(run, cap) for cap in caps], scalars, asked, shards, mpo_all
    )


def solution(mesh):
    in_specs = (
        P("sec", None, None, None),
        P("chan", None, None),
        P("chan", "sec", None, None),
        P("chan", "sec", None, None),
        P("sec"),
        P("sec"),
        P("sec", None),
        P("sec"),
    )
    out_specs = P("sec", None, "chan", None)
    return jax.shard_map(
        functools.partial(on_device, mesh.shape["chan"], mesh.shape["sec"]),
        mesh=mesh,
        in_specs=in_specs,
        out_specs=out_specs,
        check_vma=False,
    )
```

```python
import functools

import jax
import jax.numpy as jnp
from jax import lax
from jax.experimental import pallas as pl
from jax.experimental.pallas import tpu as pltpu
from jax.sharding import PartitionSpec as P

ANY = pl.BlockSpec(memory_space=pl.ANY)
SMEM = pl.BlockSpec(memory_space=pltpu.SMEM)


def after(x, *others):
    return lax.optimization_barrier((x, others))[0]


def digits(c, parity, hi, lo):
    return (c // lo, c % lo) if parity == 0 else (c % hi, c // hi)


def rank(h, l, parity, hi, lo):
    return h * lo + l if parity == 0 else l * hi + h


def left_kernel(hi, lo, where, own_dims, side_dims, own_left, side_left, *outs):
    own = outs[0].shape[1] // lo
    sectors, each = own_dims.shape[0], own_left.shape[0]
    step = pl.program_id(0)
    here, odd = where[0], where[1] == 1
    h = jnp.where(odd, here % hi, here // lo)
    l = jnp.where(odd, here // hi, here % lo)

    def fill(left, dims, at):
        for n in range(each):
            r = dims[at * each + n]
            for i in range(hi):
                for j in range(lo):
                    hh, ll = (h + i) % hi, (l + j) % lo
                    start = pl.multiple_of(jnp.where(odd, ll * hi + hh, hh * lo + ll) * own, own)
                    piece = left[n, pl.ds(start, own), :]
                    inside = (lax.broadcasted_iota(jnp.int32, piece.shape, 0) + start < r) & (
                        lax.broadcasted_iota(jnp.int32, piece.shape, 1) < r
                    )
                    outs[i][n, j * own : (j + 1) * own] = jnp.where(
                        inside, piece, jnp.zeros_like(piece)
                    )

    half = sectors // each

    @pl.when(step < half)
    def _():
        fill(own_left, own_dims, step)

    @pl.when(step >= half)
    def _():
        fill(side_left, side_dims, step - half)


def left_call(hi, lo, own_rows, where, own_dims, side_dims, own_left, side_left):
    sectors, width = own_left.shape[:2]
    each = 4 if sectors % 4 == 0 else 1
    half = sectors // each
    block = (each, lo * own_rows, width)
    return pl.pallas_call(
        functools.partial(left_kernel, hi, lo),
        grid_spec=pltpu.PrefetchScalarGridSpec(
            num_scalar_prefetch=3,
            grid=(2 * half,),
            in_specs=[
                pl.BlockSpec((each, width, width), lambda s, *_: (jnp.minimum(s, half - 1), 0, 0)),
                pl.BlockSpec((each, width, width), lambda s, *_: (jnp.maximum(s - half, 0), 0, 0)),
            ],
            out_specs=[pl.BlockSpec(block, lambda s, *_: (s, 0, 0))] * hi,
        ),
        out_shape=[jax.ShapeDtypeStruct((2 * sectors,) + block[1:], own_left.dtype)] * hi,
        compiler_params=pltpu.CompilerParams(vmem_limit_bytes=32 * 2**20),
        cost_estimate=pl.CostEstimate(
            flops=2 * own_left.size, bytes_accessed=8 * own_left.size, transcendentals=0
        ),
    )(where, own_dims, side_dims, own_left, side_left)


def plan_kernel(half, sectors, slots, me, dims, table, order, near, row, asked, seen):
    blocks = dims.shape[0]
    n_sec = table.shape[0]
    chips = n_sec // 2
    mine, parity = me[0] // 2, me[0] % 2

    def local(want):
        owner = want // sectors
        return ((owner % 2) ^ parity) * sectors + want % sectors

    def place(keep_wide):
        def body(k, at):
            fits = (dims[k] > half) == keep_wide

            @pl.when(fits)
            def _():
                order[at] = k

            return at + fits.astype(jnp.int32)

        return body

    wide = lax.fori_loop(0, blocks, place(True), jnp.int32(0))
    lax.fori_loop(0, blocks, place(False), wide)

    for chip in range(chips):
        seen[chip] = 0

    def source(k, _):
        want = table[me[0], k]
        chip = want // sectors // 2
        here = chip == mine
        count = seen[chip]
        seen[chip] = count + 1
        near[k] = here.astype(jnp.int32)
        far = ((chip ^ mine) - 1) * slots + jnp.minimum(count, slots - 1)
        row[k] = jnp.where(here, local(want), far)
        return 0

    lax.fori_loop(0, blocks, source, 0)

    for gap in range(1, chips):
        base = (gap - 1) * slots
        for n in range(slots):
            asked[base + n] = 0
        dest = (mine ^ gap) * 2 + parity

        def wish(k, count):
            want = table[dest, k]
            here = want // sectors // 2 == mine

            @pl.when(here)
            def _():
                asked[base + jnp.minimum(count, slots - 1)] = local(want)

            return count + here.astype(jnp.int32)

        lax.fori_loop(0, blocks, wish, jnp.int32(0))


def plan_call(half, sectors, slots, me, dims, table):
    blocks, chips = dims.shape[0], table.shape[0] // 2
    ints = [blocks, blocks, blocks, max(chips - 1, 1) * slots]
    return pl.pallas_call(
        functools.partial(plan_kernel, half, sectors, slots),
        in_specs=[SMEM] * 3,
        out_specs=[SMEM] * 4,
        out_shape=[jax.ShapeDtypeStruct((n,), jnp.int32) for n in ints],
        scratch_shapes=[pltpu.SMEM((chips,), jnp.int32)],
        cost_estimate=pl.CostEstimate(flops=0, bytes_accessed=4 * table.size, transcendentals=0),
    )(me, dims, table)


def block_kernel(hi, rows, narrow, first, order, right_dims, near, row, mpo, psi, *refs):
    lefts, rights = refs[: 2 * hi], refs[2 * hi : 3 * hi]
    keep, send = refs[3 * hi :]
    states = psi.shape[1]
    k = order[pl.program_id(0) + first]
    is_near = jnp.full(lefts[0].shape[1:], near[k], jnp.int32) > 0
    stacked = jnp.concatenate(
        [jnp.where(is_near, lefts[2 * i][0], lefts[2 * i + 1][0]) for i in range(hi)], axis=0
    )
    parts = [
        jnp.dot(stacked, psi[0, p], preferred_element_type=jnp.float32) for p in range(states)
    ]
    total = None
    for i in range(hi):
        right = rights[i][0]
        if not narrow:
            r = right_dims[k]
            inside = (lax.broadcasted_iota(jnp.int32, right.shape, 0) < r) & (
                lax.broadcasted_iota(jnp.int32, right.shape, 1) < r
            )
            right = jnp.where(inside, right, jnp.zeros_like(right))
        mixed = []
        for s in range(states):
            acc = None
            for p in range(states):
                piece = parts[p][i * rows : (i + 1) * rows] * mpo[i, s * states + p]
                acc = piece if acc is None else acc + piece
            mixed.append(acc.astype(jnp.bfloat16))
        mixed = jnp.concatenate(mixed, axis=0)
        product = lax.dot_general(
            mixed, right, (((1,), (1,)), ((), ())), preferred_element_type=jnp.float32
        )
        total = product if total is None else total + product
    own = keep.shape[2]
    for s in range(states):
        keep[0, s] = total[s * rows : s * rows + own].astype(keep.dtype)
        for j in range(send.shape[0]):
            at = s * rows + (j + 1) * own
            send[j, 0, s] = total[at : at + own].astype(send.dtype)


def blocks_call(hi, lo, own_rows, narrow, span, base, scalars, mpo, psi, lefts, right, others):
    states, width = psi.shape[1], psi.shape[2]
    first, count = span.start, span.stop - span.start
    across = width // 2 if narrow else width
    rows = lo * own_rows

    def by_block(k, order, *_):
        return (order[k + first], 0, 0)

    def by_row(far):
        def index(k, order, right_dims, near, row, *_):
            block = order[k + first]
            return (jnp.where(near[block] == 1 - far, row[block], 0), 0, 0)

        return index

    grid_spec = pltpu.PrefetchScalarGridSpec(
        num_scalar_prefetch=5,
        grid=(count,),
        in_specs=[
            pl.BlockSpec((1, states, width, across), lambda *at: by_block(*at) + (0,)),
        ]
        + [pl.BlockSpec((1, rows, width), by_row(far)) for _ in range(hi) for far in range(2)]
        + [pl.BlockSpec((1, across, across), by_block)]
        + [pl.BlockSpec((1, across, across), lambda k, *_: (k + first - base, 0, 0))] * (hi - 1),
        out_specs=[
            pl.BlockSpec((1, states, own_rows, across), lambda k, *_: (k, 0, 0, 0)),
            pl.BlockSpec((lo - 1, 1, states, own_rows, across), lambda k, *_: (0, k, 0, 0, 0)),
        ],
    )
    return pl.pallas_call(
        functools.partial(block_kernel, hi, rows, narrow, first),
        grid_spec=grid_spec,
        out_shape=[
            jax.ShapeDtypeStruct((count, states, own_rows, across), jnp.bfloat16),
            jax.ShapeDtypeStruct((lo - 1, count, states, own_rows, across), jnp.bfloat16),
        ],
        compiler_params=pltpu.CompilerParams(vmem_limit_bytes=40 * 2**20),
        cost_estimate=pl.CostEstimate(
            flops=count * 2 * hi * rows * states * across * (width + across),
            bytes_accessed=count * 5 * states * width * across,
            transcendentals=0,
        ),
    )(*scalars, mpo, psi, *lefts, right, *others)


def add_kernel(terms, span, order, *refs):
    out, total, sems = refs[-3:]
    across = refs[0].shape[-1]
    copies = []
    for k in range(span.stop - span.start):
        acc = refs[0][k].astype(jnp.float32)
        for j in range(1, terms):
            acc = acc + refs[j][k].astype(jnp.float32)
        total[k, :, :, :across] = acc.astype(total.dtype)
        if across < total.shape[-1]:
            total[k, :, :, across:] = jnp.zeros(acc.shape[:-1] + (total.shape[-1] - across,), total.dtype)
        copy = pltpu.make_async_copy(total.at[k], out.at[order[k + span.start]], sems.at[k])
        copy.start()
        copies.append(copy)
    for copy in copies:
        copy.wait()


def add_call(shape, span, order, terms, out):
    count = span.stop - span.start
    return pl.pallas_call(
        functools.partial(add_kernel, len(terms), span),
        in_specs=[SMEM]
        + [pl.BlockSpec(memory_space=pltpu.VMEM)] * len(terms)
        + ([] if out is None else [ANY]),
        out_specs=ANY,
        out_shape=jax.ShapeDtypeStruct(shape, jnp.bfloat16),
        scratch_shapes=[
            pltpu.VMEM((count,) + shape[1:], jnp.bfloat16),
            pltpu.SemaphoreType.DMA((count,)),
        ],
        input_output_aliases={} if out is None else {1 + len(terms): 0},
        compiler_params=pltpu.CompilerParams(vmem_limit_bytes=24 * 2**20),
        cost_estimate=pl.CostEstimate(
            flops=terms[0].size, bytes_accessed=6 * terms[0].size, transcendentals=0
        ),
    )(order, *terms, *([] if out is None else [out]))


def on_device(n_chan, n_sec, psi, mpo, left_env, right_env, left_dims, right_dims, dest_owner, left_slot):
    blocks, states, width = psi.shape[:3]
    sectors = left_env.shape[1]
    half = width // 2
    hi = 2 if n_chan % 2 == 0 else 1
    lo = n_chan // hi
    own_rows = width // n_chan
    here, me = lax.axis_index("chan"), lax.axis_index("sec")
    odd = me % 2
    right = right_env[0]
    step = max(blocks // 6, 1)

    def route(x, up, along):
        pairs = []
        for c in range(n_chan):
            for s in range(n_sec):
                h, l = digits(c, s % 2, hi, lo)
                to = rank((h + up) % hi, (l + along) % lo, s % 2, hi, lo)
                pairs.append((c * n_sec + s, to * n_sec + s))
        return lax.ppermute(x, ("chan", "sec"), pairs)

    def to_partners(x):
        return [route(x, i, 0) for i in range(1, hi)]

    def beside(x):
        return lax.ppermute(x, "sec", [(s, s ^ 1) for s in range(n_sec)])

    def fetched(x, asked):
        parts = []
        for gap in range(1, n_sec // 2):
            packed = jnp.take(x, asked[(gap - 1) * slots : gap * slots], axis=0, mode="clip")
            parts.append(lax.ppermute(packed, "sec", [(s, s ^ (2 * gap)) for s in range(n_sec)]))
        return parts

    side_left, side_dims = beside(left_env[0]), beside(left_dims)
    slots = 2 * -(-blocks // n_sec)
    wants = dest_owner[:, 0] * sectors + left_slot
    n_wide = jnp.sum((right_dims > half).astype(jnp.int32))[None]
    mine = jnp.arange(n_sec, dtype=jnp.int32)[:, None] == me
    table = lax.psum(jnp.where(mine, jnp.concatenate([wants, n_wide])[None], 0), "sec")
    most_wide = jnp.max(table[:, blocks])
    order, near, row, asked = plan_call(half, sectors, slots, me[None], right_dims, table)
    shards = left_call(
        hi, lo, own_rows, jnp.stack([here, odd]).astype(jnp.int32),
        left_dims, side_dims, left_env[0], side_left,
    )
    swapped = [route(shards[i], i, 0) for i in range(1, hi)]
    own_far = fetched(shards[0], asked)
    mpo_own = after(mpo[0], order)
    mpo_all = jnp.stack([mpo_own] + to_partners(mpo_own)).reshape(hi, states * states)
    sorted_right = jnp.take(right, order, axis=0, mode="clip")
    scalars = (order, right_dims, near, row)

    def run(cap, scalars, asked, own, own_far, swapped, sorted_right, mpo_all):
        order = scalars[0]
        spans = [(slice(a, min(a + step, cap)), False) for a in range(0, cap, step)]
        rest = blocks - cap
        count = -(-rest // (step + 1))
        for q in range(count):
            spans.append((slice(cap + rest * q // count, cap + rest * (q + 1) // count), True))
        total = len(spans)
        moved = [to_partners(sorted_right[:cap])]
        if rest:
            moved.append(to_partners(sorted_right[cap:, :half, :half]))
        lefts = [own, jnp.concatenate(own_far)]
        for x in swapped:
            lefts += [x, jnp.concatenate(fetched(x, asked))]
        shape = (blocks, states, own_rows, width)
        out, terms = None, []
        for span, narrow in spans:
            keep, send = blocks_call(
                hi, lo, own_rows, narrow, span, cap if narrow else 0, scalars, mpo_all, psi,
                lefts, right, moved[1 if narrow else 0],
            )
            if terms:
                mpo_all = after(mpo_all, keep)
            terms.append([keep] + [route(send[j - 1], 0, j) for j in range(1, lo)])
        terms[0][0] = after(terms[0][0], terms[-1][0])
        for m in range(total):
            out = add_call(shape, spans[m][0], order, terms[m], out)
        return out

    caps = sorted({max(1, blocks * q // 12) for q in (7, 8, 9)} | {blocks})
    which = sum((most_wide > cap).astype(jnp.int32) for cap in caps[:-1])
    return lax.switch(
        which, [functools.partial(run, cap) for cap in caps], scalars, asked,
        shards[0], own_far, swapped, sorted_right, mpo_all,
    )


def solution(mesh):
    in_specs = (
        P("sec", None, None, None),
        P("chan", None, None),
        P("chan", "sec", None, None),
        P("chan", "sec", None, None),
        P("sec"),
        P("sec"),
        P("sec", None),
        P("sec"),
    )
    out_specs = P("sec", None, "chan", None)
    return jax.shard_map(
        functools.partial(on_device, mesh.shape["chan"], mesh.shape["sec"]),
        mesh=mesh,
        in_specs=in_specs,
        out_specs=out_specs,
        check_vma=False,
    )
```

```python
import functools

import jax
import jax.numpy as jnp
from jax import lax
from jax.experimental import pallas as pl
from jax.experimental.pallas import tpu as pltpu
from jax.sharding import PartitionSpec as P

ANY = pl.BlockSpec(memory_space=pl.ANY)
SMEM = pl.BlockSpec(memory_space=pltpu.SMEM)


def after(x, *others):
    return lax.optimization_barrier((x, others))[0]


def digits(c, parity, hi, lo):
    return (c // lo, c % lo) if parity == 0 else (c % hi, c // hi)


def rank(h, l, parity, hi, lo):
    return h * lo + l if parity == 0 else l * hi + h


def left_kernel(hi, lo, where, own_dims, side_dims, own_left, side_left, *outs):
    own = outs[0].shape[1] // lo
    sectors, each = own_dims.shape[0], own_left.shape[0]
    step = pl.program_id(0)
    here, odd = where[0], where[1] == 1
    h = jnp.where(odd, here % hi, here // lo)
    l = jnp.where(odd, here // hi, here % lo)

    def fill(left, dims, at):
        for n in range(each):
            r = dims[at * each + n]
            for i in range(hi):
                for j in range(lo):
                    hh, ll = (h + i) % hi, (l + j) % lo
                    start = pl.multiple_of(jnp.where(odd, ll * hi + hh, hh * lo + ll) * own, own)
                    piece = left[n, pl.ds(start, own), :]
                    inside = (lax.broadcasted_iota(jnp.int32, piece.shape, 0) + start < r) & (
                        lax.broadcasted_iota(jnp.int32, piece.shape, 1) < r
                    )
                    outs[i][n, j * own : (j + 1) * own] = jnp.where(
                        inside, piece, jnp.zeros_like(piece)
                    )

    half = sectors // each

    @pl.when(step < half)
    def _():
        fill(own_left, own_dims, step)

    @pl.when(step >= half)
    def _():
        fill(side_left, side_dims, step - half)


def left_call(hi, lo, own_rows, where, own_dims, side_dims, own_left, side_left):
    sectors, width = own_left.shape[:2]
    each = 4 if sectors % 4 == 0 else 1
    half = sectors // each
    block = (each, lo * own_rows, width)
    return pl.pallas_call(
        functools.partial(left_kernel, hi, lo),
        grid_spec=pltpu.PrefetchScalarGridSpec(
            num_scalar_prefetch=3,
            grid=(2 * half,),
            in_specs=[
                pl.BlockSpec((each, width, width), lambda s, *_: (jnp.minimum(s, half - 1), 0, 0)),
                pl.BlockSpec((each, width, width), lambda s, *_: (jnp.maximum(s - half, 0), 0, 0)),
            ],
            out_specs=[pl.BlockSpec(block, lambda s, *_: (s, 0, 0))] * hi,
        ),
        out_shape=[jax.ShapeDtypeStruct((2 * sectors,) + block[1:], own_left.dtype)] * hi,
        compiler_params=pltpu.CompilerParams(vmem_limit_bytes=32 * 2**20),
        cost_estimate=pl.CostEstimate(
            flops=2 * own_left.size, bytes_accessed=8 * own_left.size, transcendentals=0
        ),
    )(where, own_dims, side_dims, own_left, side_left)


def plan_kernel(half, sectors, slots, me, dims, table, order, near, row, asked, seen):
    blocks = dims.shape[0]
    n_sec = table.shape[0]
    chips = n_sec // 2
    mine, parity = me[0] // 2, me[0] % 2

    def local(want):
        owner = want // sectors
        return ((owner % 2) ^ parity) * sectors + want % sectors

    def place(keep_wide):
        def body(k, at):
            fits = (dims[k] > half) == keep_wide

            @pl.when(fits)
            def _():
                order[at] = k

            return at + fits.astype(jnp.int32)

        return body

    wide = lax.fori_loop(0, blocks, place(True), jnp.int32(0))
    lax.fori_loop(0, blocks, place(False), wide)

    for chip in range(chips):
        seen[chip] = 0

    def source(k, _):
        want = table[me[0], k]
        chip = want // sectors // 2
        here = chip == mine
        count = seen[chip]
        seen[chip] = count + 1
        near[k] = here.astype(jnp.int32)
        far = ((chip ^ mine) - 1) * slots + jnp.minimum(count, slots - 1)
        row[k] = jnp.where(here, local(want), far)
        return 0

    lax.fori_loop(0, blocks, source, 0)

    for gap in range(1, chips):
        base = (gap - 1) * slots
        for n in range(slots):
            asked[base + n] = 0
        dest = (mine ^ gap) * 2 + parity

        def wish(k, count):
            want = table[dest, k]
            here = want // sectors // 2 == mine

            @pl.when(here)
            def _():
                asked[base + jnp.minimum(count, slots - 1)] = local(want)

            return count + here.astype(jnp.int32)

        lax.fori_loop(0, blocks, wish, jnp.int32(0))


def plan_call(half, sectors, slots, me, dims, table):
    blocks, chips = dims.shape[0], table.shape[0] // 2
    ints = [blocks, blocks, blocks, max(chips - 1, 1) * slots]
    return pl.pallas_call(
        functools.partial(plan_kernel, half, sectors, slots),
        in_specs=[SMEM] * 3,
        out_specs=[SMEM] * 4,
        out_shape=[jax.ShapeDtypeStruct((n,), jnp.int32) for n in ints],
        scratch_shapes=[pltpu.SMEM((chips,), jnp.int32)],
        cost_estimate=pl.CostEstimate(flops=0, bytes_accessed=4 * table.size, transcendentals=0),
    )(me, dims, table)


def block_kernel(hi, rows, narrow, first, order, right_dims, near, row, mpo, psi, *refs):
    lefts, rights = refs[: 2 * hi], refs[2 * hi : 3 * hi]
    keep, send = refs[3 * hi :]
    states = psi.shape[1]
    k = order[pl.program_id(0) + first]
    is_near = jnp.full(lefts[0].shape[1:], near[k], jnp.int32) > 0
    stacked = jnp.concatenate(
        [jnp.where(is_near, lefts[2 * i][0], lefts[2 * i + 1][0]) for i in range(hi)], axis=0
    )
    parts = [
        jnp.dot(stacked, psi[0, p], preferred_element_type=jnp.float32) for p in range(states)
    ]
    total = None
    for i in range(hi):
        right = rights[i][0]
        if not narrow:
            r = right_dims[k]
            inside = (lax.broadcasted_iota(jnp.int32, right.shape, 0) < r) & (
                lax.broadcasted_iota(jnp.int32, right.shape, 1) < r
            )
            right = jnp.where(inside, right, jnp.zeros_like(right))
        mixed = []
        for s in range(states):
            acc = None
            for p in range(states):
                piece = parts[p][i * rows : (i + 1) * rows] * mpo[i, s * states + p]
                acc = piece if acc is None else acc + piece
            mixed.append(acc.astype(jnp.bfloat16))
        mixed = jnp.concatenate(mixed, axis=0)
        product = lax.dot_general(
            mixed, right, (((1,), (1,)), ((), ())), preferred_element_type=jnp.float32
        )
        total = product if total is None else total + product
    own = keep.shape[2]
    for s in range(states):
        keep[0, s] = total[s * rows : s * rows + own].astype(keep.dtype)
        for j in range(send.shape[0]):
            at = s * rows + (j + 1) * own
            send[j, 0, s] = total[at : at + own].astype(send.dtype)


def blocks_call(hi, lo, own_rows, narrow, span, base, scalars, mpo, psi, lefts, right, others):
    states, width = psi.shape[1], psi.shape[2]
    first, count = span.start, span.stop - span.start
    across = width // 2 if narrow else width
    rows = lo * own_rows

    def by_block(k, order, *_):
        return (order[k + first], 0, 0)

    def by_row(far):
        def index(k, order, right_dims, near, row, *_):
            block = order[k + first]
            return (jnp.where(near[block] == 1 - far, row[block], 0), 0, 0)

        return index

    grid_spec = pltpu.PrefetchScalarGridSpec(
        num_scalar_prefetch=5,
        grid=(count,),
        in_specs=[
            pl.BlockSpec((1, states, width, across), lambda *at: by_block(*at) + (0,)),
        ]
        + [pl.BlockSpec((1, rows, width), by_row(far)) for _ in range(hi) for far in range(2)]
        + [pl.BlockSpec((1, across, across), by_block)]
        + [pl.BlockSpec((1, across, across), lambda k, *_: (k + first - base, 0, 0))] * (hi - 1),
        out_specs=[
            pl.BlockSpec((1, states, own_rows, across), lambda k, *_: (k, 0, 0, 0)),
            pl.BlockSpec((lo - 1, 1, states, own_rows, across), lambda k, *_: (0, k, 0, 0, 0)),
        ],
    )
    return pl.pallas_call(
        functools.partial(block_kernel, hi, rows, narrow, first),
        grid_spec=grid_spec,
        out_shape=[
            jax.ShapeDtypeStruct((count, states, own_rows, across), jnp.bfloat16),
            jax.ShapeDtypeStruct((lo - 1, count, states, own_rows, across), jnp.bfloat16),
        ],
        compiler_params=pltpu.CompilerParams(vmem_limit_bytes=40 * 2**20),
        cost_estimate=pl.CostEstimate(
            flops=count * 2 * hi * rows * states * across * (width + across),
            bytes_accessed=count * 5 * states * width * across,
            transcendentals=0,
        ),
    )(*scalars, mpo, psi, *lefts, right, *others)


def add_kernel(terms, span, order, *refs):
    out, total, sems = refs[-3:]
    across = refs[0].shape[-1]
    copies = []
    for k in range(span.stop - span.start):
        acc = refs[0][k].astype(jnp.float32)
        for j in range(1, terms):
            acc = acc + refs[j][k].astype(jnp.float32)
        total[k, :, :, :across] = acc.astype(total.dtype)
        if across < total.shape[-1]:
            total[k, :, :, across:] = jnp.zeros(acc.shape[:-1] + (total.shape[-1] - across,), total.dtype)
        copy = pltpu.make_async_copy(total.at[k], out.at[order[k + span.start]], sems.at[k])
        copy.start()
        copies.append(copy)
    for copy in copies:
        copy.wait()


def add_call(shape, span, order, terms, out):
    count = span.stop - span.start
    return pl.pallas_call(
        functools.partial(add_kernel, len(terms), span),
        in_specs=[SMEM]
        + [pl.BlockSpec(memory_space=pltpu.VMEM)] * len(terms)
        + ([] if out is None else [ANY]),
        out_specs=ANY,
        out_shape=jax.ShapeDtypeStruct(shape, jnp.bfloat16),
        scratch_shapes=[
            pltpu.VMEM((count,) + shape[1:], jnp.bfloat16),
            pltpu.SemaphoreType.DMA((count,)),
        ],
        input_output_aliases={} if out is None else {1 + len(terms): 0},
        compiler_params=pltpu.CompilerParams(vmem_limit_bytes=24 * 2**20),
        cost_estimate=pl.CostEstimate(
            flops=terms[0].size, bytes_accessed=6 * terms[0].size, transcendentals=0
        ),
    )(order, *terms, *([] if out is None else [out]))


def on_device(n_chan, n_sec, psi, mpo, left_env, right_env, left_dims, right_dims, dest_owner, left_slot):
    blocks, states, width = psi.shape[:3]
    sectors = left_env.shape[1]
    half = width // 2
    hi = 2 if n_chan % 2 == 0 else 1
    lo = n_chan // hi
    own_rows = width // n_chan
    here, me = lax.axis_index("chan"), lax.axis_index("sec")
    odd = me % 2
    right = right_env[0]
    step = max(blocks // 6, 1)

    def route(x, up, along):
        pairs = []
        for c in range(n_chan):
            for s in range(n_sec):
                h, l = digits(c, s % 2, hi, lo)
                to = rank((h + up) % hi, (l + along) % lo, s % 2, hi, lo)
                pairs.append((c * n_sec + s, to * n_sec + s))
        return lax.ppermute(x, ("chan", "sec"), pairs)

    def to_partners(x):
        return [route(x, i, 0) for i in range(1, hi)]

    def beside(x):
        return lax.ppermute(x, "sec", [(s, s ^ 1) for s in range(n_sec)])

    def fetched(x, asked):
        parts = []
        for gap in range(1, n_sec // 2):
            packed = jnp.take(x, asked[(gap - 1) * slots : gap * slots], axis=0, mode="clip")
            parts.append(lax.ppermute(packed, "sec", [(s, s ^ (2 * gap)) for s in range(n_sec)]))
        return parts

    side_left, side_dims = beside(left_env[0]), beside(left_dims)
    slots = 2 * -(-blocks // n_sec)
    wants = dest_owner[:, 0] * sectors + left_slot
    n_wide = jnp.sum((right_dims > half).astype(jnp.int32))[None]
    mine = jnp.arange(n_sec, dtype=jnp.int32)[:, None] == me
    table = lax.psum(jnp.where(mine, jnp.concatenate([wants, n_wide])[None], 0), "sec")
    most_wide = jnp.max(table[:, blocks])
    order, near, row, asked = plan_call(half, sectors, slots, me[None], right_dims, table)
    shards = left_call(
        hi, lo, own_rows, jnp.stack([here, odd]).astype(jnp.int32),
        left_dims, side_dims, left_env[0], side_left,
    )
    swapped = [route(shards[i], i, 0) for i in range(1, hi)]
    mpo_own = after(mpo[0], order)
    mpo_all = jnp.stack([mpo_own] + to_partners(mpo_own)).reshape(hi, states * states)
    scalars = (order, right_dims, near, row)
    caps = sorted({max(2, blocks * q // 12) for q in (7, 8, 9)} | {blocks})
    cuts = [0, min(2 * step, caps[0] - 1), caps[0]]
    first = [
        jnp.take(right, order[a:b], axis=0, mode="clip") for a, b in zip(cuts[:-1], cuts[1:])
    ]
    thin = jnp.take(right[:, :half, :half], order[caps[0] :], axis=0, mode="clip")
    first, thin = lax.optimization_barrier((first, thin, swapped))[:2]

    def run(cap, scalars, asked, shards, swapped, first, thin, mpo_all):
        order = scalars[0]
        moved = [to_partners(x) for x in first]
        bounds = list(zip(cuts[:-1], cuts[1:]))
        if cap > cuts[-1]:
            bounds.append((cuts[-1], cap))
            moved.append(to_partners(jnp.take(right, order[cuts[-1] : cap], axis=0, mode="clip")))
        spans = []
        for n, (low, high) in enumerate(bounds):
            for a in range(low, high, step):
                spans.append((slice(a, min(a + step, high)), False, low, n))
        rest = blocks - cap
        count = -(-rest // (step + 1))
        for q in range(count):
            span = slice(cap + rest * q // count, cap + rest * (q + 1) // count)
            spans.append((span, True, cap, len(moved)))
        if rest:
            moved.append(to_partners(thin[cap - caps[0] :]))
            mpo_all = after(mpo_all, moved[-1])
        total = len(spans)
        lefts = []
        for x in [shards[0]] + swapped:
            lefts += [x, jnp.concatenate(fetched(x, asked))]
        shape = (blocks, states, own_rows, width)
        out, terms = None, []
        for span, narrow, base, n in spans:
            keep, send = blocks_call(
                hi, lo, own_rows, narrow, span, base, scalars, mpo_all, psi, lefts, right, moved[n]
            )
            if terms:
                mpo_all = after(mpo_all, keep)
            terms.append([keep] + [route(send[j - 1], 0, j) for j in range(1, lo)])
        terms[0][0] = after(terms[0][0], terms[-1][0])
        for m in range(total):
            out = add_call(shape, spans[m][0], order, terms[m], out)
        return out

    which = sum((most_wide > cap).astype(jnp.int32) for cap in caps[:-1])
    return lax.switch(
        which, [functools.partial(run, cap) for cap in caps], scalars, asked,
        shards, swapped, first, thin, mpo_all,
    )


def solution(mesh):
    in_specs = (
        P("sec", None, None, None),
        P("chan", None, None),
        P("chan", "sec", None, None),
        P("chan", "sec", None, None),
        P("sec"),
        P("sec"),
        P("sec", None),
        P("sec"),
    )
    out_specs = P("sec", None, "chan", None)
    return jax.shard_map(
        functools.partial(on_device, mesh.shape["chan"], mesh.shape["sec"]),
        mesh=mesh,
        in_specs=in_specs,
        out_specs=out_specs,
        check_vma=False,
    )
```

```python
import functools

import jax
import jax.numpy as jnp
from jax import lax
from jax.experimental import pallas as pl
from jax.experimental.pallas import tpu as pltpu
from jax.sharding import PartitionSpec as P

ANY = pl.BlockSpec(memory_space=pl.ANY)
SMEM = pl.BlockSpec(memory_space=pltpu.SMEM)


def after(x, *others):
    return lax.optimization_barrier((x, others))[0]


def digits(c, parity, hi, lo):
    return (c // lo, c % lo) if parity == 0 else (c % hi, c // hi)


def rank(h, l, parity, hi, lo):
    return h * lo + l if parity == 0 else l * hi + h


def left_kernel(hi, lo, where, own_dims, side_dims, own_left, side_left, *outs):
    own = outs[0].shape[1] // lo
    sectors, each = own_dims.shape[0], own_left.shape[0]
    step = pl.program_id(0)
    here, odd = where[0], where[1] == 1
    h = jnp.where(odd, here % hi, here // lo)
    l = jnp.where(odd, here // hi, here % lo)

    def fill(left, dims, at):
        for n in range(each):
            r = dims[at * each + n]
            for i in range(hi):
                for j in range(lo):
                    hh, ll = (h + i) % hi, (l + j) % lo
                    start = pl.multiple_of(jnp.where(odd, ll * hi + hh, hh * lo + ll) * own, own)
                    piece = left[n, pl.ds(start, own), :]
                    inside = (lax.broadcasted_iota(jnp.int32, piece.shape, 0) + start < r) & (
                        lax.broadcasted_iota(jnp.int32, piece.shape, 1) < r
                    )
                    outs[i][n, j * own : (j + 1) * own] = jnp.where(
                        inside, piece, jnp.zeros_like(piece)
                    )

    half = sectors // each

    @pl.when(step < half)
    def _():
        fill(own_left, own_dims, step)

    @pl.when(step >= half)
    def _():
        fill(side_left, side_dims, step - half)


def left_call(hi, lo, own_rows, where, own_dims, side_dims, own_left, side_left):
    sectors, width = own_left.shape[:2]
    each = 4 if sectors % 4 == 0 else 1
    half = sectors // each
    block = (each, lo * own_rows, width)
    return pl.pallas_call(
        functools.partial(left_kernel, hi, lo),
        grid_spec=pltpu.PrefetchScalarGridSpec(
            num_scalar_prefetch=3,
            grid=(2 * half,),
            in_specs=[
                pl.BlockSpec((each, width, width), lambda s, *_: (jnp.minimum(s, half - 1), 0, 0)),
                pl.BlockSpec((each, width, width), lambda s, *_: (jnp.maximum(s - half, 0), 0, 0)),
            ],
            out_specs=[pl.BlockSpec(block, lambda s, *_: (s, 0, 0))] * hi,
        ),
        out_shape=[jax.ShapeDtypeStruct((2 * sectors,) + block[1:], own_left.dtype)] * hi,
        compiler_params=pltpu.CompilerParams(vmem_limit_bytes=32 * 2**20),
        cost_estimate=pl.CostEstimate(
            flops=2 * own_left.size, bytes_accessed=8 * own_left.size, transcendentals=0
        ),
    )(where, own_dims, side_dims, own_left, side_left)


def plan_kernel(half, sectors, slots, me, dims, table, order, near, row, asked, most, seen):
    blocks = dims.shape[0]
    n_sec = table.shape[0]
    chips = n_sec // 2
    mine, parity = me[0] // 2, me[0] % 2

    def local(want):
        owner = want // sectors
        return ((owner % 2) ^ parity) * sectors + want % sectors

    def place(keep_wide):
        def body(k, at):
            fits = (dims[k] > half) == keep_wide

            @pl.when(fits)
            def _():
                order[at] = k

            return at + fits.astype(jnp.int32)

        return body

    wide = lax.fori_loop(0, blocks, place(True), jnp.int32(0))
    lax.fori_loop(0, blocks, place(False), wide)

    largest = table[0, blocks]
    for s in range(1, n_sec):
        largest = jnp.maximum(largest, table[s, blocks])
    most[0] = largest

    for chip in range(chips):
        seen[chip] = 0

    def source(k, _):
        want = table[me[0], k]
        chip = want // sectors // 2
        here = chip == mine
        count = seen[chip]
        seen[chip] = count + 1
        near[k] = here.astype(jnp.int32)
        far = ((chip ^ mine) - 1) * slots + jnp.minimum(count, slots - 1)
        row[k] = jnp.where(here, local(want), far)
        return 0

    lax.fori_loop(0, blocks, source, 0)

    for gap in range(1, chips):
        base = (gap - 1) * slots
        for n in range(slots):
            asked[base + n] = 0
        dest = (mine ^ gap) * 2 + parity

        def wish(k, count):
            want = table[dest, k]
            here = want // sectors // 2 == mine

            @pl.when(here)
            def _():
                asked[base + jnp.minimum(count, slots - 1)] = local(want)

            return count + here.astype(jnp.int32)

        lax.fori_loop(0, blocks, wish, jnp.int32(0))


def plan_call(half, sectors, slots, me, dims, table):
    blocks, chips = dims.shape[0], table.shape[0] // 2
    ints = [blocks, blocks, blocks, max(chips - 1, 1) * slots, 1]
    return pl.pallas_call(
        functools.partial(plan_kernel, half, sectors, slots),
        in_specs=[SMEM] * 3,
        out_specs=[SMEM] * 5,
        out_shape=[jax.ShapeDtypeStruct((n,), jnp.int32) for n in ints],
        scratch_shapes=[pltpu.SMEM((chips,), jnp.int32)],
        cost_estimate=pl.CostEstimate(flops=0, bytes_accessed=4 * table.size, transcendentals=0),
    )(me, dims, table)


def block_kernel(hi, rows, narrow, first, order, right_dims, near, row, mpo, psi, *refs):
    lefts, rights = refs[: 2 * hi], refs[2 * hi : 3 * hi]
    keep, send = refs[3 * hi :]
    states = psi.shape[1]
    k = order[pl.program_id(0) + first]
    is_near = jnp.full(lefts[0].shape[1:], near[k], jnp.int32) > 0
    stacked = jnp.concatenate(
        [jnp.where(is_near, lefts[2 * i][0], lefts[2 * i + 1][0]) for i in range(hi)], axis=0
    )
    parts = [
        jnp.dot(stacked, psi[0, p], preferred_element_type=jnp.float32) for p in range(states)
    ]
    total = None
    for i in range(hi):
        right = rights[i][0]
        if not narrow:
            r = right_dims[k]
            inside = (lax.broadcasted_iota(jnp.int32, right.shape, 0) < r) & (
                lax.broadcasted_iota(jnp.int32, right.shape, 1) < r
            )
            right = jnp.where(inside, right, jnp.zeros_like(right))
        mixed = []
        for s in range(states):
            acc = None
            for p in range(states):
                piece = parts[p][i * rows : (i + 1) * rows] * mpo[i, s * states + p]
                acc = piece if acc is None else acc + piece
            mixed.append(acc.astype(jnp.bfloat16))
        mixed = jnp.concatenate(mixed, axis=0)
        product = lax.dot_general(
            mixed, right, (((1,), (1,)), ((), ())), preferred_element_type=jnp.float32
        )
        total = product if total is None else total + product
    own = keep.shape[2]
    for s in range(states):
        keep[0, s] = total[s * rows : s * rows + own].astype(keep.dtype)
        for j in range(send.shape[0]):
            at = s * rows + (j + 1) * own
            send[j, 0, s] = total[at : at + own].astype(send.dtype)


def blocks_call(hi, lo, own_rows, narrow, span, base, scalars, mpo, psi, lefts, right, others):
    states, width = psi.shape[1], psi.shape[2]
    first, count = span.start, span.stop - span.start
    across = width // 2 if narrow else width
    rows = lo * own_rows

    def by_block(k, order, *_):
        return (order[k + first], 0, 0)

    def by_row(far):
        def index(k, order, right_dims, near, row, *_):
            block = order[k + first]
            return (jnp.where(near[block] == 1 - far, row[block], 0), 0, 0)

        return index

    grid_spec = pltpu.PrefetchScalarGridSpec(
        num_scalar_prefetch=5,
        grid=(count,),
        in_specs=[
            pl.BlockSpec((1, states, width, across), lambda *at: by_block(*at) + (0,)),
        ]
        + [pl.BlockSpec((1, rows, width), by_row(far)) for _ in range(hi) for far in range(2)]
        + [pl.BlockSpec((1, across, across), by_block)]
        + [pl.BlockSpec((1, across, across), lambda k, *_: (k + first - base, 0, 0))] * (hi - 1),
        out_specs=[
            pl.BlockSpec((1, states, own_rows, across), lambda k, *_: (k, 0, 0, 0)),
            pl.BlockSpec((lo - 1, 1, states, own_rows, across), lambda k, *_: (0, k, 0, 0, 0)),
        ],
    )
    return pl.pallas_call(
        functools.partial(block_kernel, hi, rows, narrow, first),
        grid_spec=grid_spec,
        out_shape=[
            jax.ShapeDtypeStruct((count, states, own_rows, across), jnp.bfloat16),
            jax.ShapeDtypeStruct((lo - 1, count, states, own_rows, across), jnp.bfloat16),
        ],
        compiler_params=pltpu.CompilerParams(vmem_limit_bytes=40 * 2**20),
        cost_estimate=pl.CostEstimate(
            flops=count * 2 * hi * rows * states * across * (width + across),
            bytes_accessed=count * 5 * states * width * across,
            transcendentals=0,
        ),
    )(*scalars, mpo, psi, *lefts, right, *others)


def add_kernel(terms, span, order, *refs):
    out, total, sems = refs[-3:]
    across = refs[0].shape[-1]
    copies = []
    for k in range(span.stop - span.start):
        acc = refs[0][k].astype(jnp.float32)
        for j in range(1, terms):
            acc = acc + refs[j][k].astype(jnp.float32)
        total[k, :, :, :across] = acc.astype(total.dtype)
        if across < total.shape[-1]:
            total[k, :, :, across:] = jnp.zeros(acc.shape[:-1] + (total.shape[-1] - across,), total.dtype)
        copy = pltpu.make_async_copy(total.at[k], out.at[order[k + span.start]], sems.at[k])
        copy.start()
        copies.append(copy)
    for copy in copies:
        copy.wait()


def add_call(shape, span, order, terms, out):
    count = span.stop - span.start
    return pl.pallas_call(
        functools.partial(add_kernel, len(terms), span),
        in_specs=[SMEM]
        + [pl.BlockSpec(memory_space=pltpu.VMEM)] * len(terms)
        + ([] if out is None else [ANY]),
        out_specs=ANY,
        out_shape=jax.ShapeDtypeStruct(shape, jnp.bfloat16),
        scratch_shapes=[
            pltpu.VMEM((count,) + shape[1:], jnp.bfloat16),
            pltpu.SemaphoreType.DMA((count,)),
        ],
        input_output_aliases={} if out is None else {1 + len(terms): 0},
        compiler_params=pltpu.CompilerParams(vmem_limit_bytes=24 * 2**20),
        cost_estimate=pl.CostEstimate(
            flops=terms[0].size, bytes_accessed=6 * terms[0].size, transcendentals=0
        ),
    )(order, *terms, *([] if out is None else [out]))


def on_device(n_chan, n_sec, psi, mpo, left_env, right_env, left_dims, right_dims, dest_owner, left_slot):
    blocks, states, width = psi.shape[:3]
    sectors = left_env.shape[1]
    half = width // 2
    hi = 2 if n_chan % 2 == 0 else 1
    lo = n_chan // hi
    own_rows = width // n_chan
    here, me = lax.axis_index("chan"), lax.axis_index("sec")
    odd = me % 2
    right = right_env[0]
    step = max(blocks // 6, 1)

    def route(x, up, along):
        pairs = []
        for c in range(n_chan):
            for s in range(n_sec):
                h, l = digits(c, s % 2, hi, lo)
                to = rank((h + up) % hi, (l + along) % lo, s % 2, hi, lo)
                pairs.append((c * n_sec + s, to * n_sec + s))
        return lax.ppermute(x, ("chan", "sec"), pairs)

    def to_partners(x):
        return [route(x, i, 0) for i in range(1, hi)]

    def beside(x):
        return lax.ppermute(x, "sec", [(s, s ^ 1) for s in range(n_sec)])

    def packs(x, asked):
        return [
            jnp.take(x, asked[(gap - 1) * slots : gap * slots], axis=0, mode="clip")
            for gap in range(1, n_sec // 2)
        ]

    def over_chips(packed):
        parts = []
        for gap, x in enumerate(packed, 1):
            parts.append(lax.ppermute(x, "sec", [(s, s ^ (2 * gap)) for s in range(n_sec)]))
        return jnp.concatenate(parts)

    side_left, side_dims = beside(left_env[0]), beside(left_dims)
    slots = 2 * -(-blocks // n_sec)
    wants = dest_owner[:, 0] * sectors + left_slot
    n_wide = jnp.sum((right_dims > half).astype(jnp.int32))[None]
    mine = jnp.arange(n_sec, dtype=jnp.int32)[:, None] == me
    table = lax.psum(jnp.where(mine, jnp.concatenate([wants, n_wide])[None], 0), "sec")
    order, near, row, asked, most = plan_call(half, sectors, slots, me[None], right_dims, table)
    most_wide = most[0]
    shards = left_call(
        hi, lo, own_rows, jnp.stack([here, odd]).astype(jnp.int32),
        left_dims, side_dims, left_env[0], side_left,
    )
    swapped = [route(shards[i], i, 0) for i in range(1, hi)]
    mpo_own = after(mpo[0], order)
    mpo_all = jnp.stack([mpo_own] + to_partners(mpo_own)).reshape(hi, states * states)
    scalars = (order, right_dims, near, row)
    caps = sorted({max(2, blocks * q // 12) for q in (7, 8, 9)} | {blocks})
    first = after(jnp.take(right, order[: caps[0]], axis=0, mode="clip"), swapped)

    def run(cap, scalars, asked, shards, swapped, first, mpo_all):
        order = scalars[0]
        moved = [to_partners(first)]
        sources = [shards[0]] + swapped
        packed = [packs(x, asked) for x in sources]
        bounds = [(0, caps[0])]
        if cap > caps[0]:
            bounds.append((caps[0], cap))
            more = jnp.take(right, order[caps[0] : cap], axis=0, mode="clip")
            moved.append(to_partners(after(more, packed)))
        spans = []
        for n, (low, high) in enumerate(bounds):
            for a in range(low, high, step):
                spans.append((slice(a, min(a + step, high)), False, low, n))
        rest = blocks - cap
        count = -(-rest // (step + 1))
        for q in range(count):
            span = slice(cap + rest * q // count, cap + rest * (q + 1) // count)
            spans.append((span, True, cap, len(moved)))
        if rest:
            thin = jnp.take(right, order[cap:], axis=0, mode="clip")[:, :half, :half]
            moved.append(to_partners(after(thin, packed)))
        total = len(spans)
        lefts = []
        for x, parts in zip(sources, packed):
            lefts += [x, over_chips(parts)]
        shape = (blocks, states, own_rows, width)
        out, terms = None, []
        for span, narrow, base, n in spans:
            keep, send = blocks_call(
                hi, lo, own_rows, narrow, span, base, scalars, mpo_all, psi, lefts, right, moved[n]
            )
            mpo_all = after(mpo_all, keep, *([] if terms else moved[1:]))
            terms.append([keep] + [route(send[j - 1], 0, j) for j in range(1, lo)])
        terms[0][0] = after(terms[0][0], terms[-1][0])
        for m in range(total):
            out = add_call(shape, spans[m][0], order, terms[m], out)
        return out

    which = sum((most_wide > cap).astype(jnp.int32) for cap in caps[:-1])
    return lax.switch(
        which, [functools.partial(run, cap) for cap in caps], scalars, asked,
        shards, swapped, first, mpo_all,
    )


def solution(mesh):
    in_specs = (
        P("sec", None, None, None),
        P("chan", None, None),
        P("chan", "sec", None, None),
        P("chan", "sec", None, None),
        P("sec"),
        P("sec"),
        P("sec", None),
        P("sec"),
    )
    out_specs = P("sec", None, "chan", None)
    return jax.shard_map(
        functools.partial(on_device, mesh.shape["chan"], mesh.shape["sec"]),
        mesh=mesh,
        in_specs=in_specs,
        out_specs=out_specs,
        check_vma=False,
    )
```

```python
import functools

import jax
import jax.numpy as jnp
from jax import lax
from jax.experimental import pallas as pl
from jax.experimental.pallas import tpu as pltpu
from jax.sharding import PartitionSpec as P

ANY = pl.BlockSpec(memory_space=pl.ANY)
SMEM = pl.BlockSpec(memory_space=pltpu.SMEM)


def after(x, *others):
    return lax.optimization_barrier((x, others))[0]


def digits(c, parity, hi, lo):
    return (c // lo, c % lo) if parity == 0 else (c % hi, c // hi)


def rank(h, l, parity, hi, lo):
    return h * lo + l if parity == 0 else l * hi + h


def left_kernel(hi, lo, where, own_dims, side_dims, own_left, side_left, *outs):
    own = outs[0].shape[1] // lo
    sectors, each = own_dims.shape[0], own_left.shape[0]
    step = pl.program_id(0)
    here, odd = where[0], where[1] == 1
    h = jnp.where(odd, here % hi, here // lo)
    l = jnp.where(odd, here // hi, here % lo)

    def fill(left, dims, at):
        for n in range(each):
            r = dims[at * each + n]
            for i in range(hi):
                for j in range(lo):
                    hh, ll = (h + i) % hi, (l + j) % lo
                    start = pl.multiple_of(jnp.where(odd, ll * hi + hh, hh * lo + ll) * own, own)
                    piece = left[n, pl.ds(start, own), :]
                    inside = (lax.broadcasted_iota(jnp.int32, piece.shape, 0) + start < r) & (
                        lax.broadcasted_iota(jnp.int32, piece.shape, 1) < r
                    )
                    outs[i][n, j * own : (j + 1) * own] = jnp.where(
                        inside, piece, jnp.zeros_like(piece)
                    )

    half = sectors // each

    @pl.when(step < half)
    def _():
        fill(own_left, own_dims, step)

    @pl.when(step >= half)
    def _():
        fill(side_left, side_dims, step - half)


def left_call(hi, lo, own_rows, where, own_dims, side_dims, own_left, side_left):
    sectors, width = own_left.shape[:2]
    each = 4 if sectors % 4 == 0 else 1
    half = sectors // each
    block = (each, lo * own_rows, width)
    return pl.pallas_call(
        functools.partial(left_kernel, hi, lo),
        grid_spec=pltpu.PrefetchScalarGridSpec(
            num_scalar_prefetch=3,
            grid=(2 * half,),
            in_specs=[
                pl.BlockSpec((each, width, width), lambda s, *_: (jnp.minimum(s, half - 1), 0, 0)),
                pl.BlockSpec((each, width, width), lambda s, *_: (jnp.maximum(s - half, 0), 0, 0)),
            ],
            out_specs=[pl.BlockSpec(block, lambda s, *_: (s, 0, 0))] * hi,
        ),
        out_shape=[jax.ShapeDtypeStruct((2 * sectors,) + block[1:], own_left.dtype)] * hi,
        compiler_params=pltpu.CompilerParams(vmem_limit_bytes=32 * 2**20),
        cost_estimate=pl.CostEstimate(
            flops=2 * own_left.size, bytes_accessed=8 * own_left.size, transcendentals=0
        ),
    )(where, own_dims, side_dims, own_left, side_left)


def plan_kernel(half, sectors, slots, me, dims, table, order, near, row, asked, most, seen):
    blocks = dims.shape[0]
    n_sec = table.shape[0]
    chips = n_sec // 2
    mine, parity = me[0] // 2, me[0] % 2

    def local(want):
        owner = want // sectors
        return ((owner % 2) ^ parity) * sectors + want % sectors

    def place(keep_wide):
        def body(k, at):
            fits = (dims[k] > half) == keep_wide

            @pl.when(fits)
            def _():
                order[at] = k

            return at + fits.astype(jnp.int32)

        return body

    wide = lax.fori_loop(0, blocks, place(True), jnp.int32(0))
    lax.fori_loop(0, blocks, place(False), wide)

    largest = table[0, blocks]
    for s in range(1, n_sec):
        largest = jnp.maximum(largest, table[s, blocks])
    most[0] = largest

    for chip in range(chips):
        seen[chip] = 0

    def source(k, _):
        want = table[me[0], k]
        chip = want // sectors // 2
        here = chip == mine
        count = seen[chip]
        seen[chip] = count + 1
        near[k] = here.astype(jnp.int32)
        far = ((chip ^ mine) - 1) * slots + jnp.minimum(count, slots - 1)
        row[k] = jnp.where(here, local(want), far)
        return 0

    lax.fori_loop(0, blocks, source, 0)

    for gap in range(1, chips):
        base = (gap - 1) * slots
        for n in range(slots):
            asked[base + n] = 0
        dest = (mine ^ gap) * 2 + parity

        def wish(k, count):
            want = table[dest, k]
            here = want // sectors // 2 == mine

            @pl.when(here)
            def _():
                asked[base + jnp.minimum(count, slots - 1)] = local(want)

            return count + here.astype(jnp.int32)

        lax.fori_loop(0, blocks, wish, jnp.int32(0))


def plan_call(half, sectors, slots, me, dims, table):
    blocks, chips = dims.shape[0], table.shape[0] // 2
    ints = [blocks, blocks, blocks, max(chips - 1, 1) * slots, 1]
    return pl.pallas_call(
        functools.partial(plan_kernel, half, sectors, slots),
        in_specs=[SMEM] * 3,
        out_specs=[SMEM] * 5,
        out_shape=[jax.ShapeDtypeStruct((n,), jnp.int32) for n in ints],
        scratch_shapes=[pltpu.SMEM((chips,), jnp.int32)],
        cost_estimate=pl.CostEstimate(flops=0, bytes_accessed=4 * table.size, transcendentals=0),
    )(me, dims, table)


def pack_kernel(hi, slots, asked, *refs):
    sources, outs = refs[:hi], refs[hi:]
    rows = sources[0].shape[1]
    for gap, out in enumerate(outs):
        for n in range(slots):
            for i in range(hi):
                out[n, i * rows : (i + 1) * rows] = sources[i][asked[gap * slots + n]]


def pack_call(slots, gaps, asked, sources):
    hi = len(sources)
    _, rows, width = sources[0].shape
    vmem = pl.BlockSpec(memory_space=pltpu.VMEM)
    return pl.pallas_call(
        functools.partial(pack_kernel, hi, slots),
        in_specs=[SMEM] + [vmem] * hi,
        out_specs=[vmem] * gaps,
        out_shape=[jax.ShapeDtypeStruct((slots, hi * rows, width), sources[0].dtype)] * gaps,
        compiler_params=pltpu.CompilerParams(vmem_limit_bytes=24 * 2**20),
        cost_estimate=pl.CostEstimate(
            flops=0, bytes_accessed=4 * hi * sources[0].size, transcendentals=0
        ),
    )(asked, *sources)


def block_kernel(hi, rows, narrow, first, order, right_dims, near, row, mpo, psi, *refs):
    nears, far, rights = refs[:hi], refs[hi], refs[hi + 1 : 2 * hi + 1]
    keep, send = refs[2 * hi + 1 :]
    states = psi.shape[1]
    k = order[pl.program_id(0) + first]
    is_near = jnp.full(far.shape[1:], near[k], jnp.int32) > 0
    stacked = jnp.where(is_near, jnp.concatenate([left[0] for left in nears], axis=0), far[0])
    parts = [
        jnp.dot(stacked, psi[0, p], preferred_element_type=jnp.float32) for p in range(states)
    ]
    total = None
    for i in range(hi):
        right = rights[i][0]
        if not narrow:
            r = right_dims[k]
            inside = (lax.broadcasted_iota(jnp.int32, right.shape, 0) < r) & (
                lax.broadcasted_iota(jnp.int32, right.shape, 1) < r
            )
            right = jnp.where(inside, right, jnp.zeros_like(right))
        mixed = []
        for s in range(states):
            acc = None
            for p in range(states):
                piece = parts[p][i * rows : (i + 1) * rows] * mpo[i, s * states + p]
                acc = piece if acc is None else acc + piece
            mixed.append(acc.astype(jnp.bfloat16))
        mixed = jnp.concatenate(mixed, axis=0)
        product = lax.dot_general(
            mixed, right, (((1,), (1,)), ((), ())), preferred_element_type=jnp.float32
        )
        total = product if total is None else total + product
    own = keep.shape[2]
    for s in range(states):
        keep[0, s] = total[s * rows : s * rows + own].astype(keep.dtype)
        for j in range(send.shape[0]):
            at = s * rows + (j + 1) * own
            send[j, 0, s] = total[at : at + own].astype(send.dtype)


def blocks_call(hi, lo, own_rows, narrow, span, base, scalars, mpo, psi, lefts, right, others):
    states, width = psi.shape[1], psi.shape[2]
    first, count = span.start, span.stop - span.start
    across = width // 2 if narrow else width
    rows = lo * own_rows

    def by_block(k, order, *_):
        return (order[k + first], 0, 0)

    def by_row(far):
        def index(k, order, right_dims, near, row, *_):
            block = order[k + first]
            return (jnp.where(near[block] == 1 - far, row[block], 0), 0, 0)

        return index

    grid_spec = pltpu.PrefetchScalarGridSpec(
        num_scalar_prefetch=5,
        grid=(count,),
        in_specs=[
            pl.BlockSpec((1, states, width, across), lambda *at: by_block(*at) + (0,)),
        ]
        + [pl.BlockSpec((1, rows, width), by_row(0))] * hi
        + [pl.BlockSpec((1, hi * rows, width), by_row(1))]
        + [pl.BlockSpec((1, across, across), by_block)]
        + [pl.BlockSpec((1, across, across), lambda k, *_: (k + first - base, 0, 0))] * (hi - 1),
        out_specs=[
            pl.BlockSpec((1, states, own_rows, across), lambda k, *_: (k, 0, 0, 0)),
            pl.BlockSpec((lo - 1, 1, states, own_rows, across), lambda k, *_: (0, k, 0, 0, 0)),
        ],
    )
    return pl.pallas_call(
        functools.partial(block_kernel, hi, rows, narrow, first),
        grid_spec=grid_spec,
        out_shape=[
            jax.ShapeDtypeStruct((count, states, own_rows, across), jnp.bfloat16),
            jax.ShapeDtypeStruct((lo - 1, count, states, own_rows, across), jnp.bfloat16),
        ],
        compiler_params=pltpu.CompilerParams(vmem_limit_bytes=40 * 2**20),
        cost_estimate=pl.CostEstimate(
            flops=count * 2 * hi * rows * states * across * (width + across),
            bytes_accessed=count * 5 * states * width * across,
            transcendentals=0,
        ),
    )(*scalars, mpo, psi, *lefts, right, *others)


def add_kernel(group, order, *refs):
    out, total, sems = refs[-3:]
    copies, at = [], 0
    for span, terms in group:
        refs, parts = refs[terms:], refs[:terms]
        across = parts[0].shape[-1]
        for k in range(span.stop - span.start):
            acc = parts[0][k].astype(jnp.float32)
            for part in parts[1:]:
                acc = acc + part[k].astype(jnp.float32)
            total[at, :, :, :across] = acc.astype(total.dtype)
            if across < total.shape[-1]:
                blank = acc.shape[:-1] + (total.shape[-1] - across,)
                total[at, :, :, across:] = jnp.zeros(blank, total.dtype)
            copy = pltpu.make_async_copy(total.at[at], out.at[order[k + span.start]], sems.at[at])
            copy.start()
            copies.append(copy)
            at += 1
    for copy in copies:
        copy.wait()


def add_call(shape, order, group, out):
    count = sum(span.stop - span.start for span, _ in group)
    flat = [x for _, terms in group for x in terms]
    size = sum(x.size for x in flat)
    return pl.pallas_call(
        functools.partial(add_kernel, [(span, len(terms)) for span, terms in group]),
        in_specs=[SMEM]
        + [pl.BlockSpec(memory_space=pltpu.VMEM)] * len(flat)
        + ([] if out is None else [ANY]),
        out_specs=ANY,
        out_shape=jax.ShapeDtypeStruct(shape, jnp.bfloat16),
        scratch_shapes=[
            pltpu.VMEM((count,) + shape[1:], jnp.bfloat16),
            pltpu.SemaphoreType.DMA((count,)),
        ],
        input_output_aliases={} if out is None else {1 + len(flat): 0},
        compiler_params=pltpu.CompilerParams(vmem_limit_bytes=24 * 2**20),
        cost_estimate=pl.CostEstimate(flops=size, bytes_accessed=3 * size, transcendentals=0),
    )(order, *flat, *([] if out is None else [out]))


def on_device(n_chan, n_sec, psi, mpo, left_env, right_env, left_dims, right_dims, dest_owner, left_slot):
    blocks, states, width = psi.shape[:3]
    sectors = left_env.shape[1]
    half = width // 2
    hi = 2 if n_chan % 2 == 0 else 1
    lo = n_chan // hi
    own_rows = width // n_chan
    here, me = lax.axis_index("chan"), lax.axis_index("sec")
    odd = me % 2
    right = right_env[0]
    step = max(blocks // 6, 1)

    def route(x, up, along):
        pairs = []
        for c in range(n_chan):
            for s in range(n_sec):
                h, l = digits(c, s % 2, hi, lo)
                to = rank((h + up) % hi, (l + along) % lo, s % 2, hi, lo)
                pairs.append((c * n_sec + s, to * n_sec + s))
        return lax.ppermute(x, ("chan", "sec"), pairs)

    def to_partners(x):
        return [route(x, i, 0) for i in range(1, hi)]

    def beside(x):
        return lax.ppermute(x, "sec", [(s, s ^ 1) for s in range(n_sec)])

    def over_chips(packed):
        parts = []
        for gap, x in enumerate(packed, 1):
            parts.append(lax.ppermute(x, "sec", [(s, s ^ (2 * gap)) for s in range(n_sec)]))
        return jnp.concatenate(parts)

    side_left, side_dims = beside(left_env[0]), beside(left_dims)
    slots = 2 * -(-blocks // n_sec)
    wants = dest_owner[:, 0] * sectors + left_slot
    n_wide = jnp.sum((right_dims > half).astype(jnp.int32))[None]
    mine = jnp.arange(n_sec, dtype=jnp.int32)[:, None] == me
    table = lax.psum(jnp.where(mine, jnp.concatenate([wants, n_wide])[None], 0), "sec")
    order, near, row, asked, most = plan_call(half, sectors, slots, me[None], right_dims, table)
    most_wide = most[0]
    shards = left_call(
        hi, lo, own_rows, jnp.stack([here, odd]).astype(jnp.int32),
        left_dims, side_dims, left_env[0], side_left,
    )
    swapped = [route(shards[i], i, 0) for i in range(1, hi)]
    mpo_own = after(mpo[0], order)
    mpo_all = jnp.stack([mpo_own] + to_partners(mpo_own)).reshape(hi, states * states)
    scalars = (order, right_dims, near, row)
    caps = sorted({max(2, blocks * q // 12) for q in (7, 8, 9)} | {blocks})
    first = after(jnp.take(right, order[: caps[0]], axis=0, mode="clip"), swapped)

    def run(cap, scalars, asked, shards, swapped, first, mpo_all):
        order = scalars[0]
        moved = [to_partners(first)]
        sources = [shards[0]] + swapped
        packed = pack_call(slots, n_sec // 2 - 1, asked, sources)
        bounds = [(0, caps[0])]
        if cap > caps[0]:
            bounds.append((caps[0], cap))
            more = jnp.take(right, order[caps[0] : cap], axis=0, mode="clip")
            moved.append(to_partners(after(more, packed)))
        spans = []
        for n, (low, high) in enumerate(bounds):
            for a in range(low, high, step):
                spans.append((slice(a, min(a + step, high)), False, low, n))
        rest = blocks - cap
        count = -(-rest // (step + 1))
        for q in range(count):
            span = slice(cap + rest * q // count, cap + rest * (q + 1) // count)
            spans.append((span, True, cap, len(moved)))
        if rest:
            thin = jnp.take(right, order[cap:], axis=0, mode="clip")[:, :half, :half]
            moved.append(to_partners(after(thin, packed)))
        total = len(spans)
        lefts = sources + [over_chips(packed)]
        shape = (blocks, states, own_rows, width)
        out, terms = None, []
        for span, narrow, base, n in spans:
            keep, send = blocks_call(
                hi, lo, own_rows, narrow, span, base, scalars, mpo_all, psi, lefts, right, moved[n]
            )
            mpo_all = after(mpo_all, keep, *([] if terms else moved[1:]))
            terms.append([keep] + [route(send[j - 1], 0, j) for j in range(1, lo)])
        terms[0][0] = after(terms[0][0], terms[-1][0])
        pairs = [(span[0], term) for span, term in zip(spans, terms)]
        alone = max(total - 3, 0)
        for group in [[pair] for pair in pairs[:alone]] + [pairs[alone:]]:
            out = add_call(shape, order, group, out)
        return out

    which = sum((most_wide > cap).astype(jnp.int32) for cap in caps[:-1])
    return lax.switch(
        which, [functools.partial(run, cap) for cap in caps], scalars, asked,
        shards, swapped, first, mpo_all,
    )


def solution(mesh):
    in_specs = (
        P("sec", None, None, None),
        P("chan", None, None),
        P("chan", "sec", None, None),
        P("chan", "sec", None, None),
        P("sec"),
        P("sec"),
        P("sec", None),
        P("sec"),
    )
    out_specs = P("sec", None, "chan", None)
    return jax.shard_map(
        functools.partial(on_device, mesh.shape["chan"], mesh.shape["sec"]),
        mesh=mesh,
        in_specs=in_specs,
        out_specs=out_specs,
        check_vma=False,
    )
```

```python
import functools

import jax
import jax.numpy as jnp
from jax import lax
from jax.experimental import pallas as pl
from jax.experimental.pallas import tpu as pltpu
from jax.sharding import PartitionSpec as P

ANY = pl.BlockSpec(memory_space=pl.ANY)
SMEM = pl.BlockSpec(memory_space=pltpu.SMEM)


def after(x, *others):
    return lax.optimization_barrier((x, others))[0]


def digits(c, parity, hi, lo):
    return (c // lo, c % lo) if parity == 0 else (c % hi, c // hi)


def rank(h, l, parity, hi, lo):
    return h * lo + l if parity == 0 else l * hi + h


def left_kernel(hi, lo, where, own_dims, side_dims, own_left, side_left, *outs):
    own = outs[0].shape[1] // lo
    sectors, each = own_dims.shape[0], own_left.shape[0]
    step = pl.program_id(0)
    here, odd = where[0], where[1] == 1
    h = jnp.where(odd, here % hi, here // lo)
    l = jnp.where(odd, here // hi, here % lo)

    def fill(left, dims, at):
        for n in range(each):
            r = dims[at * each + n]
            for i in range(hi):
                for j in range(lo):
                    hh, ll = (h + i) % hi, (l + j) % lo
                    start = pl.multiple_of(jnp.where(odd, ll * hi + hh, hh * lo + ll) * own, own)
                    piece = left[n, pl.ds(start, own), :]
                    inside = (lax.broadcasted_iota(jnp.int32, piece.shape, 0) + start < r) & (
                        lax.broadcasted_iota(jnp.int32, piece.shape, 1) < r
                    )
                    outs[i][n, j * own : (j + 1) * own] = jnp.where(
                        inside, piece, jnp.zeros_like(piece)
                    )

    half = sectors // each

    @pl.when(step < half)
    def _():
        fill(own_left, own_dims, step)

    @pl.when(step >= half)
    def _():
        fill(side_left, side_dims, step - half)


def left_call(hi, lo, own_rows, where, own_dims, side_dims, own_left, side_left):
    sectors, width = own_left.shape[:2]
    each = 4 if sectors % 4 == 0 else 1
    half = sectors // each
    block = (each, lo * own_rows, width)
    return pl.pallas_call(
        functools.partial(left_kernel, hi, lo),
        grid_spec=pltpu.PrefetchScalarGridSpec(
            num_scalar_prefetch=3,
            grid=(2 * half,),
            in_specs=[
                pl.BlockSpec((each, width, width), lambda s, *_: (jnp.minimum(s, half - 1), 0, 0)),
                pl.BlockSpec((each, width, width), lambda s, *_: (jnp.maximum(s - half, 0), 0, 0)),
            ],
            out_specs=[pl.BlockSpec(block, lambda s, *_: (s, 0, 0))] * hi,
        ),
        out_shape=[jax.ShapeDtypeStruct((2 * sectors,) + block[1:], own_left.dtype)] * hi,
        compiler_params=pltpu.CompilerParams(vmem_limit_bytes=32 * 2**20),
        cost_estimate=pl.CostEstimate(
            flops=2 * own_left.size, bytes_accessed=8 * own_left.size, transcendentals=0
        ),
    )(where, own_dims, side_dims, own_left, side_left)


def plan_kernel(half, sectors, slots, me, dims, table, order, near, row, asked, most, seen):
    blocks = dims.shape[0]
    n_sec = table.shape[0]
    chips = n_sec // 2
    mine, parity = me[0] // 2, me[0] % 2

    def local(want):
        owner = want // sectors
        return ((owner % 2) ^ parity) * sectors + want % sectors

    def place(keep_wide):
        def body(k, at):
            fits = (dims[k] > half) == keep_wide

            @pl.when(fits)
            def _():
                order[at] = k

            return at + fits.astype(jnp.int32)

        return body

    wide = lax.fori_loop(0, blocks, place(True), jnp.int32(0))
    lax.fori_loop(0, blocks, place(False), wide)

    largest = table[0, blocks]
    for s in range(1, n_sec):
        largest = jnp.maximum(largest, table[s, blocks])
    most[0] = largest

    for chip in range(chips):
        seen[chip] = 0

    def source(k, _):
        want = table[me[0], k]
        chip = want // sectors // 2
        here = chip == mine
        count = seen[chip]
        seen[chip] = count + 1
        near[k] = here.astype(jnp.int32)
        far = ((chip ^ mine) - 1) * slots + jnp.minimum(count, slots - 1)
        row[k] = jnp.where(here, local(want), far)
        return 0

    lax.fori_loop(0, blocks, source, 0)

    for gap in range(1, chips):
        base = (gap - 1) * slots
        for n in range(slots):
            asked[base + n] = 0
        dest = (mine ^ gap) * 2 + parity

        def wish(k, count):
            want = table[dest, k]
            here = want // sectors // 2 == mine

            @pl.when(here)
            def _():
                asked[base + jnp.minimum(count, slots - 1)] = local(want)

            return count + here.astype(jnp.int32)

        lax.fori_loop(0, blocks, wish, jnp.int32(0))


def plan_call(half, sectors, slots, me, dims, table):
    blocks, chips = dims.shape[0], table.shape[0] // 2
    ints = [blocks, blocks, blocks, max(chips - 1, 1) * slots, 1]
    return pl.pallas_call(
        functools.partial(plan_kernel, half, sectors, slots),
        in_specs=[SMEM] * 3,
        out_specs=[SMEM] * 5,
        out_shape=[jax.ShapeDtypeStruct((n,), jnp.int32) for n in ints],
        scratch_shapes=[pltpu.SMEM((chips,), jnp.int32)],
        cost_estimate=pl.CostEstimate(flops=0, bytes_accessed=4 * table.size, transcendentals=0),
    )(me, dims, table)


def pack_kernel(hi, slots, asked, *refs):
    sources, outs = refs[:hi], refs[hi:]
    rows = sources[0].shape[1]
    for gap, out in enumerate(outs):
        for n in range(slots):
            for i in range(hi):
                out[n, i * rows : (i + 1) * rows] = sources[i][asked[gap * slots + n]]


def pack_call(slots, gaps, asked, sources):
    hi = len(sources)
    _, rows, width = sources[0].shape
    vmem = pl.BlockSpec(memory_space=pltpu.VMEM)
    return pl.pallas_call(
        functools.partial(pack_kernel, hi, slots),
        in_specs=[SMEM] + [vmem] * hi,
        out_specs=[vmem] * gaps,
        out_shape=[jax.ShapeDtypeStruct((slots, hi * rows, width), sources[0].dtype)] * gaps,
        compiler_params=pltpu.CompilerParams(vmem_limit_bytes=24 * 2**20),
        cost_estimate=pl.CostEstimate(
            flops=0, bytes_accessed=4 * hi * sources[0].size, transcendentals=0
        ),
    )(asked, *sources)


def block_kernel(hi, rows, narrow, first, order, right_dims, near, row, mpo, psi, *refs):
    nears, far, rights = refs[:hi], refs[hi], refs[hi + 1 : 2 * hi + 1]
    keep, send = refs[2 * hi + 1 :]
    states = psi.shape[1]
    k = order[pl.program_id(0) + first]
    is_near = jnp.full(far.shape[1:], near[k], jnp.int32) > 0
    stacked = jnp.where(is_near, jnp.concatenate([left[0] for left in nears], axis=0), far[0])
    parts = [
        jnp.dot(stacked, psi[0, p], preferred_element_type=jnp.float32) for p in range(states)
    ]
    total = None
    for i in range(hi):
        right = rights[i][0]
        if not narrow:
            r = right_dims[k]
            inside = (lax.broadcasted_iota(jnp.int32, right.shape, 0) < r) & (
                lax.broadcasted_iota(jnp.int32, right.shape, 1) < r
            )
            right = jnp.where(inside, right, jnp.zeros_like(right))
        mixed = []
        for s in range(states):
            acc = None
            for p in range(states):
                piece = parts[p][i * rows : (i + 1) * rows] * mpo[i, s * states + p]
                acc = piece if acc is None else acc + piece
            mixed.append(acc.astype(jnp.bfloat16))
        mixed = jnp.concatenate(mixed, axis=0)
        product = lax.dot_general(
            mixed, right, (((1,), (1,)), ((), ())), preferred_element_type=jnp.float32
        )
        total = product if total is None else total + product
    own = keep.shape[2]
    for s in range(states):
        keep[0, s] = total[s * rows : s * rows + own].astype(keep.dtype)
        for j in range(send.shape[0]):
            at = s * rows + (j + 1) * own
            send[j, 0, s] = total[at : at + own].astype(send.dtype)


def blocks_call(hi, lo, own_rows, narrow, span, base, scalars, mpo, psi, lefts, right, others):
    states, width = psi.shape[1], psi.shape[2]
    first, count = span.start, span.stop - span.start
    across = width // 2 if narrow else width
    rows = lo * own_rows

    def by_block(k, order, *_):
        return (order[k + first], 0, 0)

    def by_row(far):
        def index(k, order, right_dims, near, row, *_):
            block = order[k + first]
            return (jnp.where(near[block] == 1 - far, row[block], 0), 0, 0)

        return index

    grid_spec = pltpu.PrefetchScalarGridSpec(
        num_scalar_prefetch=5,
        grid=(count,),
        in_specs=[
            pl.BlockSpec((1, states, width, across), lambda *at: by_block(*at) + (0,)),
        ]
        + [pl.BlockSpec((1, rows, width), by_row(0))] * hi
        + [pl.BlockSpec((1, hi * rows, width), by_row(1))]
        + [pl.BlockSpec((1, across, across), by_block)]
        + [pl.BlockSpec((1, across, across), lambda k, *_: (k + first - base, 0, 0))] * (hi - 1),
        out_specs=[
            pl.BlockSpec((1, states, own_rows, across), lambda k, *_: (k, 0, 0, 0)),
            pl.BlockSpec((lo - 1, 1, states, own_rows, across), lambda k, *_: (0, k, 0, 0, 0)),
        ],
    )
    return pl.pallas_call(
        functools.partial(block_kernel, hi, rows, narrow, first),
        grid_spec=grid_spec,
        out_shape=[
            jax.ShapeDtypeStruct((count, states, own_rows, across), jnp.bfloat16),
            jax.ShapeDtypeStruct((lo - 1, count, states, own_rows, across), jnp.bfloat16),
        ],
        compiler_params=pltpu.CompilerParams(vmem_limit_bytes=40 * 2**20),
        cost_estimate=pl.CostEstimate(
            flops=count * 2 * hi * rows * states * across * (width + across),
            bytes_accessed=count * 5 * states * width * across,
            transcendentals=0,
        ),
    )(*scalars, mpo, psi, *lefts, right, *others)


def add_kernel(group, order, *refs):
    out, total, sems = refs[-3:]
    copies, at = [], 0
    for span, terms in group:
        refs, parts = refs[terms:], refs[:terms]
        across = parts[0].shape[-1]
        for k in range(span.stop - span.start):
            acc = parts[0][k].astype(jnp.float32)
            for part in parts[1:]:
                acc = acc + part[k].astype(jnp.float32)
            total[at, :, :, :across] = acc.astype(total.dtype)
            if across < total.shape[-1]:
                blank = acc.shape[:-1] + (total.shape[-1] - across,)
                total[at, :, :, across:] = jnp.zeros(blank, total.dtype)
            copy = pltpu.make_async_copy(total.at[at], out.at[order[k + span.start]], sems.at[at])
            copy.start()
            copies.append(copy)
            at += 1
    for copy in copies:
        copy.wait()


def add_call(shape, order, group, out):
    count = sum(span.stop - span.start for span, _ in group)
    flat = [x for _, terms in group for x in terms]
    size = sum(x.size for x in flat)
    return pl.pallas_call(
        functools.partial(add_kernel, [(span, len(terms)) for span, terms in group]),
        in_specs=[SMEM]
        + [pl.BlockSpec(memory_space=pltpu.VMEM)] * len(flat)
        + ([] if out is None else [ANY]),
        out_specs=ANY,
        out_shape=jax.ShapeDtypeStruct(shape, jnp.bfloat16),
        scratch_shapes=[
            pltpu.VMEM((count,) + shape[1:], jnp.bfloat16),
            pltpu.SemaphoreType.DMA((count,)),
        ],
        input_output_aliases={} if out is None else {1 + len(flat): 0},
        compiler_params=pltpu.CompilerParams(vmem_limit_bytes=24 * 2**20),
        cost_estimate=pl.CostEstimate(flops=size, bytes_accessed=3 * size, transcendentals=0),
    )(order, *flat, *([] if out is None else [out]))


def on_device(n_chan, n_sec, psi, mpo, left_env, right_env, left_dims, right_dims, dest_owner, left_slot):
    blocks, states, width = psi.shape[:3]
    sectors = left_env.shape[1]
    half = width // 2
    hi = 2 if n_chan % 2 == 0 else 1
    lo = n_chan // hi
    own_rows = width // n_chan
    here, me = lax.axis_index("chan"), lax.axis_index("sec")
    odd = me % 2
    right = right_env[0]
    step = max(blocks // 6, 1)

    def route(x, up, along):
        pairs = []
        for c in range(n_chan):
            for s in range(n_sec):
                h, l = digits(c, s % 2, hi, lo)
                to = rank((h + up) % hi, (l + along) % lo, s % 2, hi, lo)
                pairs.append((c * n_sec + s, to * n_sec + s))
        return lax.ppermute(x, ("chan", "sec"), pairs)

    def to_partners(x):
        return [route(x, i, 0) for i in range(1, hi)]

    def beside(x):
        return lax.ppermute(x, "sec", [(s, s ^ 1) for s in range(n_sec)])

    def over_chips(packed):
        parts = []
        for gap, x in enumerate(packed, 1):
            parts.append(lax.ppermute(x, "sec", [(s, s ^ (2 * gap)) for s in range(n_sec)]))
        return jnp.concatenate(parts)

    side_left, side_dims = beside(left_env[0]), beside(left_dims)
    slots = 2 * -(-blocks // n_sec)
    wants = dest_owner[:, 0] * sectors + left_slot
    n_wide = jnp.sum((right_dims > half).astype(jnp.int32))[None]
    mine = jnp.arange(n_sec, dtype=jnp.int32)[:, None] == me
    table = lax.psum(jnp.where(mine, jnp.concatenate([wants, n_wide])[None], 0), "sec")
    order, near, row, asked, most = plan_call(half, sectors, slots, me[None], right_dims, table)
    most_wide = most[0]
    shards = left_call(
        hi, lo, own_rows, jnp.stack([here, odd]).astype(jnp.int32),
        left_dims, side_dims, left_env[0], side_left,
    )
    swapped = [route(shards[i], i, 0) for i in range(1, hi)]
    mpo_own = after(mpo[0], order)
    mpo_all = jnp.stack([mpo_own] + to_partners(mpo_own)).reshape(hi, states * states)
    scalars = (order, right_dims, near, row)
    caps = sorted({max(2, blocks * q // 12) for q in (7, 8, 9, 10)} | {blocks})
    first = after(jnp.take(right, order[: caps[0]], axis=0, mode="clip"), swapped)

    def run(cap, scalars, asked, shards, swapped, first, mpo_all):
        order = scalars[0]
        moved = [to_partners(first)]
        sources = [shards[0]] + swapped
        packed = pack_call(slots, n_sec // 2 - 1, asked, sources)
        bounds = [(0, caps[0])]
        if cap > caps[0]:
            bounds.append((caps[0], cap))
            more = jnp.take(right, order[caps[0] : cap], axis=0, mode="clip")
            moved.append(to_partners(after(more, packed)))
        spans = []
        for n, (low, high) in enumerate(bounds):
            for a in range(low, high, step):
                spans.append((slice(a, min(a + step, high)), False, low, n))
        rest = blocks - cap
        count = -(-rest // (step + 1))
        for q in range(count):
            span = slice(cap + rest * q // count, cap + rest * (q + 1) // count)
            spans.append((span, True, cap, len(moved)))
        if rest:
            thin = jnp.take(right, order[cap:], axis=0, mode="clip")[:, :half, :half]
            moved.append(to_partners(after(thin, packed)))
        total = len(spans)
        lefts = sources + [over_chips(packed)]
        shape = (blocks, states, own_rows, width)
        out, terms = None, []
        for span, narrow, base, n in spans:
            keep, send = blocks_call(
                hi, lo, own_rows, narrow, span, base, scalars, mpo_all, psi, lefts, right, moved[n]
            )
            if not terms:
                send = after(send, *moved[1:])
            mpo_all = after(mpo_all, keep, *([] if terms else moved[1:]))
            terms.append([keep] + [route(send[j - 1], 0, j) for j in range(1, lo)])
        terms[0][0] = after(terms[0][0], terms[-1][0])
        pairs = [(span[0], term) for span, term in zip(spans, terms)]
        alone = max(total - 3, 0)
        for group in [[pair] for pair in pairs[:alone]] + [pairs[alone:]]:
            out = add_call(shape, order, group, out)
        return out

    which = sum((most_wide > cap).astype(jnp.int32) for cap in caps[:-1])
    return lax.switch(
        which, [functools.partial(run, cap) for cap in caps], scalars, asked,
        shards, swapped, first, mpo_all,
    )


def solution(mesh):
    in_specs = (
        P("sec", None, None, None),
        P("chan", None, None),
        P("chan", "sec", None, None),
        P("chan", "sec", None, None),
        P("sec"),
        P("sec"),
        P("sec", None),
        P("sec"),
    )
    out_specs = P("sec", None, "chan", None)
    return jax.shard_map(
        functools.partial(on_device, mesh.shape["chan"], mesh.shape["sec"]),
        mesh=mesh,
        in_specs=in_specs,
        out_specs=out_specs,
        check_vma=False,
    )
```

```python
import functools

import jax
import jax.numpy as jnp
from jax import lax
from jax.experimental import pallas as pl
from jax.experimental.pallas import tpu as pltpu
from jax.sharding import PartitionSpec as P

ANY = pl.BlockSpec(memory_space=pl.ANY)
SMEM = pl.BlockSpec(memory_space=pltpu.SMEM)


def after(x, *others):
    return lax.optimization_barrier((x, others))[0]


def digits(c, parity, hi, lo):
    return (c // lo, c % lo) if parity == 0 else (c % hi, c // hi)


def rank(h, l, parity, hi, lo):
    return h * lo + l if parity == 0 else l * hi + h


def left_kernel(hi, lo, where, own_dims, side_dims, own_left, side_left, *outs):
    own = outs[0].shape[1] // lo
    sectors, each = own_dims.shape[0], own_left.shape[0]
    step = pl.program_id(0)
    here, odd = where[0], where[1] == 1
    h = jnp.where(odd, here % hi, here // lo)
    l = jnp.where(odd, here // hi, here % lo)

    def fill(left, dims, at):
        for n in range(each):
            r = dims[at * each + n]
            for i in range(hi):
                for j in range(lo):
                    hh, ll = (h + i) % hi, (l + j) % lo
                    start = pl.multiple_of(jnp.where(odd, ll * hi + hh, hh * lo + ll) * own, own)
                    piece = left[n, pl.ds(start, own), :]
                    inside = (lax.broadcasted_iota(jnp.int32, piece.shape, 0) + start < r) & (
                        lax.broadcasted_iota(jnp.int32, piece.shape, 1) < r
                    )
                    outs[i][n, j * own : (j + 1) * own] = jnp.where(
                        inside, piece, jnp.zeros_like(piece)
                    )

    half = sectors // each

    @pl.when(step < half)
    def _():
        fill(own_left, own_dims, step)

    @pl.when(step >= half)
    def _():
        fill(side_left, side_dims, step - half)


def left_call(hi, lo, own_rows, where, own_dims, side_dims, own_left, side_left):
    sectors, width = own_left.shape[:2]
    each = 4 if sectors % 4 == 0 else 1
    half = sectors // each
    block = (each, lo * own_rows, width)
    return pl.pallas_call(
        functools.partial(left_kernel, hi, lo),
        grid_spec=pltpu.PrefetchScalarGridSpec(
            num_scalar_prefetch=3,
            grid=(2 * half,),
            in_specs=[
                pl.BlockSpec((each, width, width), lambda s, *_: (jnp.minimum(s, half - 1), 0, 0)),
                pl.BlockSpec((each, width, width), lambda s, *_: (jnp.maximum(s - half, 0), 0, 0)),
            ],
            out_specs=[pl.BlockSpec(block, lambda s, *_: (s, 0, 0))] * hi,
        ),
        out_shape=[jax.ShapeDtypeStruct((2 * sectors,) + block[1:], own_left.dtype)] * hi,
        compiler_params=pltpu.CompilerParams(vmem_limit_bytes=32 * 2**20),
        cost_estimate=pl.CostEstimate(
            flops=2 * own_left.size, bytes_accessed=8 * own_left.size, transcendentals=0
        ),
    )(where, own_dims, side_dims, own_left, side_left)


def plan_kernel(half, sectors, slots, me, dims, table, order, near, row, asked, most, seen):
    blocks = dims.shape[0]
    n_sec = table.shape[0]
    chips = n_sec // 2
    mine, parity = me[0] // 2, me[0] % 2

    def local(want):
        owner = want // sectors
        return ((owner % 2) ^ parity) * sectors + want % sectors

    def place(keep_wide):
        def body(k, at):
            fits = (dims[k] > half) == keep_wide

            @pl.when(fits)
            def _():
                order[at] = k

            return at + fits.astype(jnp.int32)

        return body

    wide = lax.fori_loop(0, blocks, place(True), jnp.int32(0))
    lax.fori_loop(0, blocks, place(False), wide)

    largest = table[0, blocks]
    for s in range(1, n_sec):
        largest = jnp.maximum(largest, table[s, blocks])
    most[0] = largest

    for chip in range(chips):
        seen[chip] = 0

    def source(k, _):
        want = table[me[0], k]
        chip = want // sectors // 2
        here = chip == mine
        count = seen[chip]
        seen[chip] = count + 1
        near[k] = here.astype(jnp.int32)
        far = ((chip ^ mine) - 1) * slots + jnp.minimum(count, slots - 1)
        row[k] = jnp.where(here, local(want), far)
        return 0

    lax.fori_loop(0, blocks, source, 0)

    for gap in range(1, chips):
        base = (gap - 1) * slots
        for n in range(slots):
            asked[base + n] = 0
        dest = (mine ^ gap) * 2 + parity

        def wish(k, count):
            want = table[dest, k]
            here = want // sectors // 2 == mine

            @pl.when(here)
            def _():
                asked[base + jnp.minimum(count, slots - 1)] = local(want)

            return count + here.astype(jnp.int32)

        lax.fori_loop(0, blocks, wish, jnp.int32(0))


def plan_call(half, sectors, slots, me, dims, table):
    blocks, chips = dims.shape[0], table.shape[0] // 2
    ints = [blocks, blocks, blocks, max(chips - 1, 1) * slots, 1]
    return pl.pallas_call(
        functools.partial(plan_kernel, half, sectors, slots),
        in_specs=[SMEM] * 3,
        out_specs=[SMEM] * 5,
        out_shape=[jax.ShapeDtypeStruct((n,), jnp.int32) for n in ints],
        scratch_shapes=[pltpu.SMEM((chips,), jnp.int32)],
        cost_estimate=pl.CostEstimate(flops=0, bytes_accessed=4 * table.size, transcendentals=0),
    )(me, dims, table)


def block_kernel(hi, rows, narrow, first, order, right_dims, near, row, mpo, psi, *refs):
    lefts, rights = refs[: 2 * hi], refs[2 * hi : 3 * hi]
    keep, send = refs[3 * hi :]
    states = psi.shape[1]
    k = order[pl.program_id(0) + first]
    is_near = jnp.full(lefts[0].shape[1:], near[k], jnp.int32) > 0
    stacked = jnp.concatenate(
        [jnp.where(is_near, lefts[2 * i][0], lefts[2 * i + 1][0]) for i in range(hi)], axis=0
    )
    parts = [
        jnp.dot(stacked, psi[0, p], preferred_element_type=jnp.float32) for p in range(states)
    ]
    total = None
    for i in range(hi):
        right = rights[i][0]
        if not narrow:
            r = right_dims[k]
            inside = (lax.broadcasted_iota(jnp.int32, right.shape, 0) < r) & (
                lax.broadcasted_iota(jnp.int32, right.shape, 1) < r
            )
            right = jnp.where(inside, right, jnp.zeros_like(right))
        mixed = []
        for s in range(states):
            acc = None
            for p in range(states):
                piece = parts[p][i * rows : (i + 1) * rows] * mpo[i, s * states + p]
                acc = piece if acc is None else acc + piece
            mixed.append(acc.astype(jnp.bfloat16))
        mixed = jnp.concatenate(mixed, axis=0)
        product = lax.dot_general(
            mixed, right, (((1,), (1,)), ((), ())), preferred_element_type=jnp.float32
        )
        total = product if total is None else total + product
    own = keep.shape[2]
    for s in range(states):
        keep[0, s] = total[s * rows : s * rows + own].astype(keep.dtype)
        for j in range(send.shape[0]):
            at = s * rows + (j + 1) * own
            send[j, 0, s] = total[at : at + own].astype(send.dtype)


def blocks_call(hi, lo, own_rows, narrow, span, base, scalars, mpo, psi, lefts, right, others):
    states, width = psi.shape[1], psi.shape[2]
    first, count = span.start, span.stop - span.start
    across = width // 2 if narrow else width
    rows = lo * own_rows

    def by_block(k, order, *_):
        return (order[k + first], 0, 0)

    def by_row(far):
        def index(k, order, right_dims, near, row, *_):
            block = order[k + first]
            return (jnp.where(near[block] == 1 - far, row[block], 0), 0, 0)

        return index

    grid_spec = pltpu.PrefetchScalarGridSpec(
        num_scalar_prefetch=5,
        grid=(count,),
        in_specs=[
            pl.BlockSpec((1, states, width, across), lambda *at: by_block(*at) + (0,)),
        ]
        + [pl.BlockSpec((1, rows, width), by_row(far)) for _ in range(hi) for far in range(2)]
        + [pl.BlockSpec((1, across, across), by_block)]
        + [pl.BlockSpec((1, across, across), lambda k, *_: (k + first - base, 0, 0))] * (hi - 1),
        out_specs=[
            pl.BlockSpec((1, states, own_rows, across), lambda k, *_: (k, 0, 0, 0)),
            pl.BlockSpec((lo - 1, 1, states, own_rows, across), lambda k, *_: (0, k, 0, 0, 0)),
        ],
    )
    return pl.pallas_call(
        functools.partial(block_kernel, hi, rows, narrow, first),
        grid_spec=grid_spec,
        out_shape=[
            jax.ShapeDtypeStruct((count, states, own_rows, across), jnp.bfloat16),
            jax.ShapeDtypeStruct((lo - 1, count, states, own_rows, across), jnp.bfloat16),
        ],
        compiler_params=pltpu.CompilerParams(vmem_limit_bytes=40 * 2**20),
        cost_estimate=pl.CostEstimate(
            flops=count * 2 * hi * rows * states * across * (width + across),
            bytes_accessed=count * 5 * states * width * across,
            transcendentals=0,
        ),
    )(*scalars, mpo, psi, *lefts, right, *others)


def add_kernel(group, order, *refs):
    out, total, sems = refs[-3:]
    copies, at = [], 0
    for span, terms in group:
        refs, parts = refs[terms:], refs[:terms]
        across = parts[0].shape[-1]
        for k in range(span.stop - span.start):
            acc = parts[0][k].astype(jnp.float32)
            for part in parts[1:]:
                acc = acc + part[k].astype(jnp.float32)
            total[at, :, :, :across] = acc.astype(total.dtype)
            if across < total.shape[-1]:
                blank = acc.shape[:-1] + (total.shape[-1] - across,)
                total[at, :, :, across:] = jnp.zeros(blank, total.dtype)
            copy = pltpu.make_async_copy(total.at[at], out.at[order[k + span.start]], sems.at[at])
            copy.start()
            copies.append(copy)
            at += 1
    for copy in copies:
        copy.wait()


def add_call(shape, order, group, out):
    count = sum(span.stop - span.start for span, _ in group)
    flat = [x for _, terms in group for x in terms]
    size = sum(x.size for x in flat)
    return pl.pallas_call(
        functools.partial(add_kernel, [(span, len(terms)) for span, terms in group]),
        in_specs=[SMEM]
        + [pl.BlockSpec(memory_space=pltpu.VMEM)] * len(flat)
        + ([] if out is None else [ANY]),
        out_specs=ANY,
        out_shape=jax.ShapeDtypeStruct(shape, jnp.bfloat16),
        scratch_shapes=[
            pltpu.VMEM((count,) + shape[1:], jnp.bfloat16),
            pltpu.SemaphoreType.DMA((count,)),
        ],
        input_output_aliases={} if out is None else {1 + len(flat): 0},
        compiler_params=pltpu.CompilerParams(vmem_limit_bytes=24 * 2**20),
        cost_estimate=pl.CostEstimate(flops=size, bytes_accessed=3 * size, transcendentals=0),
    )(order, *flat, *([] if out is None else [out]))


def on_device(n_chan, n_sec, psi, mpo, left_env, right_env, left_dims, right_dims, dest_owner, left_slot):
    blocks, states, width = psi.shape[:3]
    sectors = left_env.shape[1]
    half = width // 2
    hi = 2 if n_chan % 2 == 0 else 1
    lo = n_chan // hi
    own_rows = width // n_chan
    here, me = lax.axis_index("chan"), lax.axis_index("sec")
    odd = me % 2
    right = right_env[0]
    step = max(blocks // 6, 1)

    def route(x, up, along):
        pairs = []
        for c in range(n_chan):
            for s in range(n_sec):
                h, l = digits(c, s % 2, hi, lo)
                to = rank((h + up) % hi, (l + along) % lo, s % 2, hi, lo)
                pairs.append((c * n_sec + s, to * n_sec + s))
        return lax.ppermute(x, ("chan", "sec"), pairs)

    def to_partners(x):
        return [route(x, i, 0) for i in range(1, hi)]

    def beside(x):
        return lax.ppermute(x, "sec", [(s, s ^ 1) for s in range(n_sec)])

    def packs(x, asked):
        return [
            jnp.take(x, asked[(gap - 1) * slots : gap * slots], axis=0, mode="clip")
            for gap in range(1, n_sec // 2)
        ]

    def over_chips(packed):
        parts = []
        for gap, x in enumerate(packed, 1):
            parts.append(lax.ppermute(x, "sec", [(s, s ^ (2 * gap)) for s in range(n_sec)]))
        return jnp.concatenate(parts)

    side_left, side_dims = beside(left_env[0]), beside(left_dims)
    slots = 2 * -(-blocks // n_sec)
    wants = dest_owner[:, 0] * sectors + left_slot
    n_wide = jnp.sum((right_dims > half).astype(jnp.int32))[None]
    mine = jnp.arange(n_sec, dtype=jnp.int32)[:, None] == me
    table = lax.psum(jnp.where(mine, jnp.concatenate([wants, n_wide])[None], 0), "sec")
    order, near, row, asked, most = plan_call(half, sectors, slots, me[None], right_dims, table)
    most_wide = most[0]
    shards = left_call(
        hi, lo, own_rows, jnp.stack([here, odd]).astype(jnp.int32),
        left_dims, side_dims, left_env[0], side_left,
    )
    swapped = [route(shards[i], i, 0) for i in range(1, hi)]
    mpo_own = after(mpo[0], order)
    mpo_all = jnp.stack([mpo_own] + to_partners(mpo_own)).reshape(hi, states * states)
    scalars = (order, right_dims, near, row)
    caps = sorted({max(2, blocks * q // 12) for q in (7, 8, 9, 10)} | {blocks})
    first = after(jnp.take(right, order[: caps[0]], axis=0, mode="clip"), swapped)

    def run(cap, scalars, asked, shards, swapped, first, mpo_all):
        order = scalars[0]
        moved = [to_partners(first)]
        sources = [shards[0]] + swapped
        packed = [packs(x, asked) for x in sources]
        bounds = [(0, caps[0])]
        if cap > caps[0]:
            bounds.append((caps[0], cap))
            more = jnp.take(right, order[caps[0] : cap], axis=0, mode="clip")
            moved.append(to_partners(after(more, packed)))
        spans = []
        for n, (low, high) in enumerate(bounds):
            for a in range(low, high, step):
                spans.append((slice(a, min(a + step, high)), False, low, n))
        rest = blocks - cap
        count = -(-rest // (step + 1))
        for q in range(count):
            span = slice(cap + rest * q // count, cap + rest * (q + 1) // count)
            spans.append((span, True, cap, len(moved)))
        if rest:
            thin = jnp.take(right, order[cap:], axis=0, mode="clip")[:, :half, :half]
            moved.append(to_partners(after(thin, packed)))
        total = len(spans)
        lefts = []
        for x, parts in zip(sources, packed):
            lefts += [x, over_chips(parts)]
        shape = (blocks, states, own_rows, width)
        out, terms = None, []
        for span, narrow, base, n in spans:
            keep, send = blocks_call(
                hi, lo, own_rows, narrow, span, base, scalars, mpo_all, psi, lefts, right, moved[n]
            )
            mpo_all = after(mpo_all, keep, *([] if terms else moved[1:]))
            terms.append([keep] + [route(send[j - 1], 0, j) for j in range(1, lo)])
        terms[0][0] = after(terms[0][0], terms[-1][0])
        pairs = [(span[0], term) for span, term in zip(spans, terms)]
        alone = max(total - 3, 0)
        for group in [[pair] for pair in pairs[:alone]] + [pairs[alone:]]:
            out = add_call(shape, order, group, out)
        return out

    which = sum((most_wide > cap).astype(jnp.int32) for cap in caps[:-1])
    return lax.switch(
        which, [functools.partial(run, cap) for cap in caps], scalars, asked,
        shards, swapped, first, mpo_all,
    )


def solution(mesh):
    in_specs = (
        P("sec", None, None, None),
        P("chan", None, None),
        P("chan", "sec", None, None),
        P("chan", "sec", None, None),
        P("sec"),
        P("sec"),
        P("sec", None),
        P("sec"),
    )
    out_specs = P("sec", None, "chan", None)
    return jax.shard_map(
        functools.partial(on_device, mesh.shape["chan"], mesh.shape["sec"]),
        mesh=mesh,
        in_specs=in_specs,
        out_specs=out_specs,
        check_vma=False,
    )
```
